32 devices in a mesh: dp: 2 (over core), seq: 4 (over y, x), tensor: 4 (over z).
Axes of the slice: x: 2, y: 2, z: 4, core: 2. Of those that a mesh axis runs over, the one named last changes fastest.
Arguments:
- query_rows: bfloat16 [2, 768, 3072], P('dp', 'seq', 'tensor'), may hold values from -12 to 12
- key_rows: bfloat16 [2, 768, 3072], P('dp', 'seq', 'tensor'), may hold values from -12 to 12
- value_rows: bfloat16 [2, 768, 3072], P('dp', 'seq', 'tensor'), may hold values from -6 to 6
- lengths: int32 [2], P('dp'), may hold values from 384 to 768, as said below
- out_weight: bfloat16 [3072, 3072], P('seq', 'tensor'), may hold values from -4.1875 to 4.1875
- gate_vector: float32 [2, 3072], P('dp'), may hold values from 0.5 to 1.5
- cotangent: bfloat16 [2, 768, 3072], P('dp', 'seq', 'tensor'), may hold values from -12 to 12
Outputs:
- branch_out: bfloat16 [2, 768, 3072], P('dp', 'seq', 'tensor')
- grad_query: bfloat16 [2, 768, 3072], P('dp', 'seq', 'tensor')
- grad_key: bfloat16 [2, 768, 3072], P('dp', 'seq', 'tensor')
- grad_value: bfloat16 [2, 768, 3072], P('dp', 'seq', 'tensor')
- grad_weight: float32 [3072, 3072], P('seq', 'tensor')
- grad_gate: float32 [2, 3072], P('dp', 'tensor')
The draws below stay inside these ranges and needn't reach their ends.
Inputs may be any that keep to these rules, and one draw needn't show every extreme that they name: `lengths`: some clip has all 768 positions live.
All inputs are finite; a program needn't handle non-finite values.
Results may differ from the reference program's by a relative error of at most 0.035.
Values may be sent and summed in bfloat16 or wider, within the bound.
No kernel may reach another device: no remote copies, remote signals or barrier semaphores. Data moves between devices by JAX's collectives and lax.ppermute only.
A program may use at most 64 MiB of HBM per device.

```python
import math
import jax
import jax.numpy as jnp
from jax import lax

D = 3072
HEADS = 24
HD = 128
CLIPS = 2
SEQ_LEN = 768


def drawn_pair(key):
    streams = jax.random.split(jax.random.fold_in(key, 101), 2)
    full_shape = (CLIPS, SEQ_LEN, D)
    query_mat = jnp.clip(jax.random.normal(streams[0], full_shape, jnp.float32), -6.0, 6.0)
    key_mat = jnp.clip(jax.random.normal(streams[1], full_shape, jnp.float32), -6.0, 6.0)
    return (query_mat, key_mat)


def draw_query_rows(key, part):
    return drawn_pair(key)[0].astype(jnp.bfloat16)


def draw_key_rows(key, part):
    return drawn_pair(key)[1].astype(jnp.bfloat16)


def draw_lengths(key, part):
    streams = jax.random.split(jax.random.fold_in(key, 202), 2)
    drawn_lengths = jax.random.randint(streams[0], (CLIPS,), SEQ_LEN // 2, SEQ_LEN + 1)
    full_clip = jax.random.randint(streams[1], (), 0, CLIPS)
    return jnp.where(jnp.arange(CLIPS) == full_clip, SEQ_LEN, drawn_lengths).astype(jnp.int32)


def draw_cotangent(key, part):
    streams = jax.random.split(jax.random.fold_in(key, 303), 1)
    full_shape = (CLIPS, SEQ_LEN, D)
    token_ramp = 1.0 + 2.0 * jnp.arange(SEQ_LEN, dtype=jnp.float32)[None, :, None] / (SEQ_LEN - 1)
    noise_part = jnp.clip(jax.random.normal(streams[0], full_shape, jnp.float32), -4.0, 4.0)
    return (noise_part * token_ramp).astype(jnp.bfloat16)


def level_of(rng, dims, shards, least, top_value):
    factor_of, own = 1.0, jax.random.fold_in(rng, 6)
    for position, shards_of in shards:
        steps = jnp.exp(jax.random.uniform(jax.random.fold_in(own, position), (shards_of,), jnp.float32, least / len(shards), top_value / len(shards)))
        factor_of = factor_of * jnp.repeat(steps, dims[position] // shards_of).reshape([-1 if axis == position else 1 for axis in range(len(dims))])
    return factor_of


def noise(key, extent, deviation, bound, cuts=(), kind=jnp.bfloat16):
    level = level_of(key, extent, cuts, -0.22, 0.18) if cuts else 1.0
    result = jax.random.normal(key, extent, jnp.float32) * deviation * level
    return jnp.minimum(jnp.maximum(result, -bound), bound).astype(kind)


def setup_inputs(seed: int = 0) -> dict:
    keys = jax.random.split(jax.random.key(seed), 8)
    query_rows = draw_query_rows(jax.random.fold_in(keys[7], 71), 0)
    key_rows = draw_key_rows(jax.random.fold_in(keys[7], 71), 0)
    value_rows = noise(keys[2], (CLIPS, SEQ_LEN, D), 1.0, 6.0, ((0, 2), (1, 4), (2, 4)))
    lengths = draw_lengths(jax.random.fold_in(keys[7], 71), 0)
    out_weight = noise(keys[4], (D, D), 0.7, 4.1875, ((0, 4), (1, 4)))
    gate_vector = jnp.clip(0.5 + 1.0 * jax.random.uniform(keys[5], (CLIPS, D), jnp.float32) ** level_of(keys[5], (CLIPS, D), ((0, 2),), -0.2, 0.2), 0.5, 1.5)
    cotangent = draw_cotangent(jax.random.fold_in(keys[7], 71), 0)
    return dict(query_rows=query_rows, key_rows=key_rows, value_rows=value_rows, lengths=lengths, out_weight=out_weight, gate_vector=gate_vector, cotangent=cotangent)


MASKED_SCORE = -1e+30

def to_heads(array):
    return array.reshape(CLIPS, SEQ_LEN, HEADS, HD).transpose(0, 2, 1, 3).reshape(CLIPS * HEADS, SEQ_LEN, HD)

def from_heads(array):
    return array.reshape(CLIPS, HEADS, SEQ_LEN, HD).transpose(0, 2, 1, 3).reshape(CLIPS, SEQ_LEN, D)

def head_forward(record):
    query_mat, key_mat, value_mat, length = record
    key_live = jnp.arange(SEQ_LEN) < length
    scores = jnp.dot(query_mat, key_mat.T, preferred_element_type=jnp.float32) * (1.0 / math.sqrt(HD))
    masked = jnp.where(key_live[None, :], scores, MASKED_SCORE)
    row_top = lax.optimization_barrier(jnp.max(masked, axis=1))
    weights = jnp.where(key_live[None, :], jnp.exp(masked - row_top[:, None]), 0.0)
    row_total = lax.optimization_barrier(jnp.sum(weights, axis=1))
    summed = jnp.dot(weights.astype(jnp.bfloat16), value_mat, preferred_element_type=jnp.float32)
    attended = (summed / row_total[:, None]).astype(jnp.bfloat16)
    return (attended, row_top + jnp.log(row_total))

def head_backward(record):
    query_mat, key_mat, value_mat, attended, grad_att, lse, length = record
    score_scale = 1.0 / math.sqrt(HD)
    key_live = jnp.arange(SEQ_LEN) < length
    scores = jnp.dot(query_mat, key_mat.T, preferred_element_type=jnp.float32) * score_scale
    probs = jnp.where(key_live[None, :], jnp.exp(scores - lse[:, None]), 0.0)
    row_delta = lax.optimization_barrier(jnp.sum(grad_att.astype(jnp.float32) * attended.astype(jnp.float32), axis=1))
    grad_probs = jnp.dot(grad_att, value_mat.T, preferred_element_type=jnp.float32)
    dscores = (probs * (grad_probs - row_delta[:, None]) * score_scale).astype(jnp.bfloat16)
    grad_value = jnp.dot(probs.astype(jnp.bfloat16).T, grad_att, preferred_element_type=jnp.float32).astype(jnp.bfloat16)
    grad_query = jnp.dot(dscores, key_mat, preferred_element_type=jnp.float32).astype(jnp.bfloat16)
    grad_key = jnp.dot(dscores.T, query_mat, preferred_element_type=jnp.float32).astype(jnp.bfloat16)
    return (grad_query, grad_key, grad_value)

def reference(query_rows, key_rows, value_rows, lengths, out_weight, gate_vector, cotangent):
    query_items = to_heads(query_rows)
    key_items = to_heads(key_rows)
    value_items = to_heads(value_rows)
    length_items = jnp.repeat(lengths, HEADS)
    attended_items, lse_items = lax.map(head_forward, (query_items, key_items, value_items, length_items))
    attended = from_heads(attended_items)

    def clip_step(running, record):
        clip_att, gate_row, cot_rows = record
        projected = jnp.dot(clip_att, out_weight.T, preferred_element_type=jnp.float32)
        branch = (gate_row[None, :] * projected).astype(jnp.bfloat16)
        gate_grad = lax.optimization_barrier(jnp.sum(cot_rows.astype(jnp.float32) * projected, axis=0))
        grad_proj = (gate_row[None, :] * cot_rows.astype(jnp.float32)).astype(jnp.bfloat16)
        grad_att = jnp.dot(grad_proj, out_weight, preferred_element_type=jnp.float32).astype(jnp.bfloat16)
        running = running + jnp.dot(grad_proj.T, clip_att, preferred_element_type=jnp.float32)
        return (running, (branch, gate_grad, grad_att))
    grad_weight, (branch_out, grad_gate, grad_attended) = lax.scan(clip_step, jnp.zeros((D, D), jnp.float32), (attended, gate_vector, cotangent))
    grad_items = lax.map(head_backward, (query_items, key_items, value_items, attended_items, to_heads(grad_attended), lse_items, length_items))
    grad_query = from_heads(grad_items[0])
    grad_key = from_heads(grad_items[1])
    grad_value = from_heads(grad_items[2])
    return (branch_out, grad_query, grad_key, grad_value, grad_weight, grad_gate)
```

```python
import functools
import math

import jax
import jax.numpy as jnp
from jax import lax
from jax.experimental import pallas as pl
from jax.experimental.pallas import tpu as pltpu
from jax.sharding import PartitionSpec as P

HD = 128


MASKED_SCORE = -1e30


def block_rows(piece_rows):
    return math.gcd(piece_rows, 512)


def query_terms(
    query_heads, grad_heads, row_lse, row_delta, key_block, value_block, key_live, score_scale
):
    scores = (
        jnp.einsum("thd,shd->ths", query_heads, key_block, preferred_element_type=jnp.float32)
        * score_scale
    )
    probs = jnp.where(key_live[None, None, :], jnp.exp(scores - row_lse[:, :, None]), 0.0)
    grad_probs = jnp.einsum(
        "thd,shd->ths", grad_heads, value_block, preferred_element_type=jnp.float32
    )
    dscores = (probs * (grad_probs - row_delta[:, :, None]) * score_scale).astype(jnp.bfloat16)
    return jnp.einsum("ths,shd->thd", dscores, key_block, preferred_element_type=jnp.float32)


def key_terms(
    query_block, grad_block, lse_block, delta_block, key_heads, value_heads, key_live, score_scale
):
    scores = (
        jnp.einsum("shd,thd->sht", query_block, key_heads, preferred_element_type=jnp.float32)
        * score_scale
    )
    probs = jnp.where(key_live[None, None, :], jnp.exp(scores - lse_block[:, :, None]), 0.0)
    value_part = jnp.einsum(
        "sht,shd->thd", probs.astype(jnp.bfloat16), grad_block, preferred_element_type=jnp.float32
    )
    grad_probs = jnp.einsum(
        "shd,thd->sht", grad_block, value_heads, preferred_element_type=jnp.float32
    )
    dscores = (probs * (grad_probs - delta_block[:, :, None]) * score_scale).astype(jnp.bfloat16)
    key_part = jnp.einsum("sht,shd->thd", dscores, query_block, preferred_element_type=jnp.float32)
    return (key_part, value_part)


def general_shards(query_rows, key_rows, value_rows, lengths, out_weight, gate_vector, cotangent):
    tokens = query_rows.shape[1]
    local_width = query_rows.shape[2]
    head_count = local_width // HD
    score_scale = 1.0 / math.sqrt(HD)
    length = lengths[0]
    query_local = query_rows[0]
    key_local = key_rows[0]
    value_local = value_rows[0]
    query_heads = query_local.reshape(tokens, head_count, HD)
    key_heads = key_local.reshape(tokens, head_count, HD)
    value_heads = value_local.reshape(tokens, head_count, HD)
    head_zeros = jnp.zeros((tokens, head_count, HD), jnp.float32)
    start_top = jnp.full((tokens, head_count), MASKED_SCORE, jnp.float32)
    start_total = jnp.zeros((tokens, head_count), jnp.float32)
    key_piece = lax.all_gather(key_local, "seq", axis=0, tiled=True)
    value_piece = lax.all_gather(value_local, "seq", axis=0, tiled=True)
    piece_rows = key_piece.shape[0]
    step_rows = block_rows(piece_rows)

    def forward_block_step(block_index, state):
        row_top, row_total, summed = state
        offset = block_index * step_rows
        key_block = lax.dynamic_slice_in_dim(key_piece, offset, step_rows, 0).reshape(
            step_rows, head_count, HD
        )
        value_block = lax.dynamic_slice_in_dim(value_piece, offset, step_rows, 0).reshape(
            step_rows, head_count, HD
        )
        key_live = offset + jnp.arange(step_rows) < length
        scores = (
            jnp.einsum("thd,shd->ths", query_heads, key_block, preferred_element_type=jnp.float32)
            * score_scale
        )
        masked = jnp.where(key_live[None, None, :], scores, MASKED_SCORE)
        new_top = jnp.maximum(row_top, jnp.max(masked, axis=2))
        weights = jnp.where(key_live[None, None, :], jnp.exp(masked - new_top[:, :, None]), 0.0)
        shrink = jnp.exp(row_top - new_top)
        row_total = row_total * shrink + jnp.sum(weights, axis=2)
        summed = summed * shrink[:, :, None] + jnp.einsum(
            "ths,shd->thd",
            weights.astype(jnp.bfloat16),
            value_block,
            preferred_element_type=jnp.float32,
        )
        return (new_top, row_total, summed)

    row_top, row_total, summed = lax.fori_loop(
        0, piece_rows // step_rows, forward_block_step, (start_top, start_total, head_zeros)
    )
    attended_heads = (summed / row_total[:, :, None]).astype(jnp.bfloat16)
    attended = attended_heads.reshape(tokens, local_width)
    row_lse = row_top + jnp.log(row_total)
    weight_whole = lax.all_gather(out_weight, "seq", axis=0, tiled=True)
    partial_value = jnp.einsum(
        "tk,rk->tr", attended, weight_whole, preferred_element_type=jnp.float32
    )
    projected = lax.psum_scatter(
        partial_value.astype(jnp.bfloat16), "tensor", scatter_dimension=1, tiled=True
    ).astype(jnp.float32)
    out_width = projected.shape[1]
    gate_local = lax.dynamic_slice_in_dim(
        gate_vector[0], lax.axis_index("tensor") * out_width, out_width
    )
    cot_rows = cotangent[0].astype(jnp.float32)
    branch = (gate_local[None, :] * projected).astype(jnp.bfloat16)
    gate_grad = lax.psum(jnp.sum(cot_rows * projected, axis=0), "seq")
    grad_proj = (gate_local[None, :] * cot_rows).astype(jnp.bfloat16)
    grad_full = lax.all_gather(grad_proj, "tensor", axis=1, tiled=True)
    grad_att = jnp.dot(grad_full, weight_whole, preferred_element_type=jnp.float32).astype(
        jnp.bfloat16
    )
    row_share = lax.psum_scatter(
        jnp.einsum("tr,tk->rk", grad_full, attended, preferred_element_type=jnp.float32).astype(
            jnp.bfloat16
        ),
        "seq",
        scatter_dimension=0,
        tiled=True,
    )
    grad_weight = lax.psum(row_share, "dp").astype(jnp.float32)
    grad_heads = grad_att.reshape(tokens, head_count, HD)
    row_delta = jnp.sum(grad_heads.astype(jnp.float32) * attended_heads.astype(jnp.float32), axis=2)
    all_lse, all_delta = (
        lax.all_gather(row_lse, "seq", axis=0, tiled=True),
        lax.all_gather(row_delta, "seq", axis=0, tiled=True),
    )
    key_offset = lax.axis_index("seq") * tokens
    local_live = key_offset + jnp.arange(tokens) < length
    query_key_piece = lax.all_gather(key_local, "seq", axis=0, tiled=True)
    query_value_piece = lax.all_gather(value_local, "seq", axis=0, tiled=True)
    piece_rows = query_key_piece.shape[0]
    query_step_rows = block_rows(piece_rows)

    def query_block_step(block_index, state):
        offset = block_index * query_step_rows
        key_block = lax.dynamic_slice_in_dim(query_key_piece, offset, query_step_rows, 0).reshape(
            query_step_rows, head_count, HD
        )
        value_block = lax.dynamic_slice_in_dim(
            query_value_piece, offset, query_step_rows, 0
        ).reshape(query_step_rows, head_count, HD)
        key_live = offset + jnp.arange(query_step_rows) < length
        return state + query_terms(
            query_heads,
            grad_heads,
            row_lse,
            row_delta,
            key_block,
            value_block,
            key_live,
            score_scale,
        )

    grad_q = lax.fori_loop(0, piece_rows // query_step_rows, query_block_step, head_zeros)
    query_piece = lax.all_gather(query_local, "seq", axis=0, tiled=True)
    grad_piece = lax.all_gather(grad_att, "seq", axis=0, tiled=True)
    piece_rows = query_piece.shape[0]
    key_step_rows = block_rows(piece_rows)

    def key_block_step(block_index, state):
        offset = block_index * key_step_rows
        query_block = lax.dynamic_slice_in_dim(query_piece, offset, key_step_rows, 0).reshape(
            key_step_rows, head_count, HD
        )
        grad_block = lax.dynamic_slice_in_dim(grad_piece, offset, key_step_rows, 0).reshape(
            key_step_rows, head_count, HD
        )
        lse_block = lax.dynamic_slice_in_dim(all_lse, offset, key_step_rows, 0)
        delta_block = lax.dynamic_slice_in_dim(all_delta, offset, key_step_rows, 0)
        key_part, value_part = key_terms(
            query_block,
            grad_block,
            lse_block,
            delta_block,
            key_heads,
            value_heads,
            local_live,
            score_scale,
        )
        return (state[0] + key_part, state[1] + value_part)

    grad_k, grad_v = lax.fori_loop(
        0, piece_rows // key_step_rows, key_block_step, (head_zeros, head_zeros)
    )
    grad_query = grad_q.reshape(tokens, local_width).astype(jnp.bfloat16)
    grad_key = grad_k.reshape(tokens, local_width).astype(jnp.bfloat16)
    grad_value = grad_v.reshape(tokens, local_width).astype(jnp.bfloat16)
    return (
        branch[None],
        grad_query[None],
        grad_key[None],
        grad_value[None],
        grad_weight,
        gate_grad[None],
    )


VMEM_LIMIT = 40 * 1024 * 1024
NT = (((1,), (1,)), ((), ()))
TN = (((0,), (0,)), ((), ()))
NN = (((1,), (0,)), ((), ()))


def mm(left, right, dims):
    return lax.dot_general(left, right, dims, preferred_element_type=jnp.float32)


def lane_block(index, width):
    return pl.ds(pl.multiple_of(index * width, HD), width)


def call(kernel, out_shape, args, flops=0, smem=(), scratch=()):
    nbytes = sum(a.size * a.dtype.itemsize for a in args)
    nbytes += sum(math.prod(o.shape) * o.dtype.itemsize for o in jax.tree.leaves(out_shape))
    return pl.pallas_call(
        kernel,
        out_shape=out_shape,
        in_specs=[
            pl.BlockSpec(memory_space=pltpu.SMEM if i in smem else pltpu.VMEM)
            for i in range(len(args))
        ],
        out_specs=jax.tree.map(lambda _: pl.BlockSpec(memory_space=pltpu.VMEM), out_shape),
        scratch_shapes=list(scratch),
        compiler_params=pltpu.CompilerParams(vmem_limit_bytes=VMEM_LIMIT),
        cost_estimate=pl.CostEstimate(flops=flops, bytes_accessed=nbytes, transcendentals=0),
    )(*args)


def xor_pairs(count, k):
    return [(i, i ^ k) for i in range(count)]


def pack_kernel(n, q_ref, k_ref, v_ref, *out_refs):
    s = lax.axis_index("seq")
    half = q_ref.shape[1] // 2
    for k in range(n):
        j = s ^ k
        own = lane_block(j, HD)
        shared = lane_block(n + j // 2, HD)
        out = out_refs[k]
        for i in range(2):
            rows = slice(i * half, (i + 1) * half)
            out[i] = k_ref[0, rows, own]
            out[2 + i] = k_ref[0, rows, shared]
            out[4 + i] = v_ref[0, rows, own]
            out[6 + i] = v_ref[0, rows, shared]
            out[8 + i] = q_ref[0, rows, own]
        out[10] = q_ref[0, pl.ds(pl.multiple_of((j % 2) * half, half), half), shared]


def rows_of(packs, first):
    return jnp.concatenate([p[first + i] for p in packs for i in range(2)], axis=0)


def unit_queries(packs, unit):
    if unit < 2:
        return rows_of(packs[2 * unit : 2 * unit + 2], 8)
    return jnp.concatenate([p[10] for p in packs], axis=0)


def live_bias(s, n, rows, length):
    parts = []
    for k in range(n):
        place = (s ^ k) * rows + lax.broadcasted_iota(jnp.int32, (rows, 1), 0)
        parts.append(jnp.where(place < length, 0.0, MASKED_SCORE))
    return jnp.concatenate(parts, axis=0)


def forward_kernel(n, scale, len_ref, *refs):
    packs, (o_ref, lse_ref) = refs[:n], refs[n:]
    s, t = lax.axis_index("seq"), lax.axis_index("tensor")
    half = packs[0].shape[1]
    bias = live_bias(s, n, 2 * half, len_ref[0])
    for unit in range(3):
        keys = rows_of(packs, 0 if unit < 2 else 2)
        values = rows_of(packs, 4 if unit < 2 else 6)
        scores = mm(keys, unit_queries(packs, unit), NT) * scale + bias
        top = jnp.max(scores, axis=0, keepdims=True)
        weights = jnp.exp(scores - top)
        total = jnp.sum(weights, axis=0, keepdims=True)
        summed = mm(values, weights.astype(jnp.bfloat16), TN)
        attended = (summed / total).T.astype(jnp.bfloat16)
        lse_ref[unit : unit + 1, :] = top + jnp.log(total)
        if unit < 2:
            for i in range(2):
                slot = (s ^ (2 * unit + i)) ^ t
                for h in range(2):
                    at = (2 * i + h) * half
                    o_ref[slot, h] = attended[at : at + half]
        else:
            for k in range(n):
                o_ref[(s ^ k) ^ t, 2] = attended[k * half : (k + 1) * half]


def grad_attended_kernel(n, gate_ref, w_ref, *refs):
    cots, (gp_ref, *out_refs) = refs[:n], refs[n:]
    s = lax.axis_index("seq")
    rows = cots[0].shape[1]
    half = rows // 2
    gate = gate_ref[:, lane_block(s, w_ref.shape[0])]
    for i in range(n):
        gp_ref[i * rows : (i + 1) * rows, :] = (gate * cots[i][0].astype(jnp.float32)).astype(
            jnp.bfloat16
        )
    full = mm(gp_ref[...], w_ref[...], NN).astype(jnp.bfloat16)
    share = refs[-1]
    share[...] = full
    for k in range(n):
        j = s ^ k
        own = lane_block(j, HD)
        shared = lane_block(n + j // 2, HD)
        out = out_refs[k]
        for i in range(n):
            for h in range(2):
                out[i, h] = share[i * rows + h * half : i * rows + (h + 1) * half, own]
            out[i, 2] = share[pl.ds(pl.multiple_of(i * rows + (j % 2) * half, half), half), shared]


def backward_kernel(n, scale, len_ref, lse_ref, o_ref, *refs):
    packs, grads, outs = refs[:n], refs[n : 2 * n], refs[2 * n :]
    s, t = lax.axis_index("seq"), lax.axis_index("tensor")
    half = packs[0].shape[1]
    bias = live_bias(s, n, 2 * half, len_ref[0])

    def grad_tile(slot, tile):
        total = grads[0][slot, tile].astype(jnp.float32)
        for g in grads[1:]:
            total = total + g[slot, tile].astype(jnp.float32)
        return total.astype(jnp.bfloat16)

    for head in range(2):
        units = (0, 1) if head == 0 else (2,)
        keys = rows_of(packs, 2 * head)
        values = rows_of(packs, 4 + 2 * head)
        keys_t = keys.T
        grad_keys = grad_values = None
        for unit in units:
            queries = unit_queries(packs, unit)
            if unit < 2:
                tiles = [((s ^ (2 * unit + i)) ^ t, h) for i in range(2) for h in range(2)]
            else:
                tiles = [((s ^ k) ^ t, 2) for k in range(n)]
            grad = jnp.concatenate([grad_tile(*tile) for tile in tiles], axis=0)
            attended = jnp.concatenate([o_ref[slot, tile] for slot, tile in tiles], axis=0)
            product = grad.astype(jnp.float32) * attended.astype(jnp.float32)
            delta = jnp.sum(product.T, axis=0, keepdims=True)
            scores = mm(keys, queries, NT) * scale + bias
            probs = jnp.exp(scores - lse_ref[unit : unit + 1, :])
            grad_probs = mm(values, grad, NT)
            dscores = (probs * (grad_probs - delta) * scale).astype(jnp.bfloat16)
            value_part = mm(probs.astype(jnp.bfloat16), grad, NN)
            key_part = mm(dscores, queries, NN)
            grad_values = value_part if grad_values is None else grad_values + value_part
            grad_keys = key_part if grad_keys is None else grad_keys + key_part
            grad_query = mm(keys_t, dscores, NN).T.astype(jnp.bfloat16)
            if unit < 2:
                for i in range(2):
                    for h in range(2):
                        at = (2 * i + h) * half
                        outs[2 * unit + i][8 + h] = grad_query[at : at + half]
            else:
                for k in range(n):
                    outs[k][10] = grad_query[k * half : (k + 1) * half]
        for k in range(n):
            for h in range(2):
                rows = slice((2 * k + h) * half, (2 * k + h + 1) * half)
                outs[k][2 * head + h] = grad_keys[rows].astype(jnp.bfloat16)
                outs[k][4 + 2 * head + h] = grad_values[rows].astype(jnp.bfloat16)


def unpack_kernel(n, *refs):
    packs, (dq_ref, dk_ref, dv_ref) = refs[:n], refs[n:]
    s = lax.axis_index("seq")
    half = packs[0].shape[1]
    for k in range(n):
        own = lane_block(s ^ k, HD)
        for h in range(2):
            rows = slice(h * half, (h + 1) * half)
            dk_ref[0, rows, own] = packs[k][h]
            dv_ref[0, rows, own] = packs[k][4 + h]
            dq_ref[0, rows, own] = packs[k][8 + h]
    for pair in range(0, n, 2):
        shared = lane_block(n + (s ^ pair) // 2, HD)
        for h in range(2):
            rows = slice(h * half, (h + 1) * half)
            for first, ref in ((2, dk_ref), (6, dv_ref)):
                total = packs[pair][first + h].astype(jnp.float32)
                total = total + packs[pair + 1][first + h].astype(jnp.float32)
                ref[0, rows, shared] = total.astype(jnp.bfloat16)
        for k in (pair, pair + 1):
            rows = pl.ds(pl.multiple_of(((s ^ k) % 2) * half, half), half)
            dq_ref[0, rows, shared] = packs[k][10]


def project_kernel(n, w_ref, *refs):
    packs, (own_ref, *send_refs), all_ref = refs[:n], refs[n : 2 * n], refs[2 * n]
    s = lax.axis_index("seq")
    half = packs[0].shape[2]
    rows = 2 * half
    for k in range(n):
        j = s ^ k
        own = lane_block(j, HD)
        shared = lane_block(n + j // 2, HD)
        for i in range(n):
            for h in range(2):
                at = i * rows + h * half
                all_ref[at : at + half, own] = packs[k][i, h]
            at = pl.multiple_of(i * rows + (j % 2) * half, half)
            all_ref[pl.ds(at, half), shared] = packs[k][i, 2]
    weight = w_ref[...]
    for i in range(n):
        part = mm(all_ref[i * rows : (i + 1) * rows, :], weight, NT)
        if i == 0:
            own_ref[...] = part
        else:
            send_refs[i - 1][...] = part.astype(jnp.bfloat16)


def grad_weight_kernel(gp_ref, all_ref, out_ref):
    out_ref[...] = mm(gp_ref[...], all_ref[...], TN).astype(jnp.bfloat16)


def branch_kernel(n, gate_ref, cot_ref, own_ref, *refs):
    parts, (branch_ref, gate_grad_ref) = refs[: n - 1], refs[n - 1 :]
    s = lax.axis_index("seq")
    projected = own_ref[...]
    for part in parts:
        projected = projected + part[...].astype(jnp.float32)
    gate = gate_ref[:, lane_block(s, projected.shape[1])]
    branch_ref[0] = (gate * projected).astype(jnp.bfloat16)
    gate_grad_ref[...] = jnp.sum(cot_ref[0].astype(jnp.float32) * projected, axis=0, keepdims=True)


def square_shards(
    n, query_rows, key_rows, value_rows, lengths, out_weight, gate_vector, cotangent
):
    tokens, width = query_rows.shape[1:]
    half = tokens // 2
    scale = 1.0 / math.sqrt(HD)
    bf16, f32 = jnp.bfloat16, jnp.float32
    shape = jax.ShapeDtypeStruct
    both = ("seq", "tensor")

    cots = [
        lax.ppermute(
            cotangent,
            both,
            [(a * n + b, b * n + (a ^ k)) for a in range(n) for b in range(n)],
        )
        for k in range(n)
    ]
    packs = call(
        functools.partial(pack_kernel, n),
        [shape((11, half, HD), bf16)] * n,
        (query_rows, key_rows, value_rows),
    )
    packs = [packs[0]] + [lax.ppermute(packs[k], "seq", xor_pairs(n, k)) for k in range(1, n)]
    unit_flops = 2 * n * tokens * 2 * tokens * HD
    attended, lse = call(
        functools.partial(forward_kernel, n, scale),
        [shape((n, 3, half, HD), bf16), shape((3, 2 * tokens), f32)],
        (lengths, *packs),
        flops=6 * unit_flops,
        smem=(0,),
    )
    heads = [attended] + [lax.ppermute(attended, "seq", xor_pairs(n, k)) for k in range(1, n)]
    grad_proj, *grads = call(
        functools.partial(grad_attended_kernel, n),
        [shape((n * tokens, width), bf16)] + [shape((n, 3, half, HD), bf16)] * n,
        (gate_vector, out_weight, *cots),
        flops=2 * n * tokens * width * width,
        scratch=[pltpu.VMEM((n * tokens, width), bf16)],
    )
    grads = [grads[0]] + [lax.ppermute(grads[k], "seq", xor_pairs(n, k)) for k in range(1, n)]
    *parts, attended_all = call(
        functools.partial(project_kernel, n),
        [shape((tokens, width), f32)]
        + [shape((tokens, width), bf16)] * (n - 1)
        + [shape((n * tokens, width), bf16)],
        (out_weight, *heads),
        flops=2 * n * tokens * width * width,
    )
    parts = [parts[0]] + [lax.ppermute(parts[k], "tensor", xor_pairs(n, k)) for k in range(1, n)]
    weight_part = call(
        grad_weight_kernel,
        shape((width, width), bf16),
        (grad_proj, attended_all),
        flops=2 * n * tokens * width * width,
    )
    other_part = lax.ppermute(weight_part, "dp", xor_pairs(2, 1))
    grad_weight = weight_part.astype(f32) + other_part.astype(f32)
    outs = call(
        functools.partial(backward_kernel, n, scale),
        [shape((11, half, HD), bf16)] * n,
        (lengths, lse, attended, *packs, *grads),
        flops=15 * unit_flops,
        smem=(0,),
    )
    outs = [outs[0]] + [lax.ppermute(outs[k], "seq", xor_pairs(n, k)) for k in range(1, n)]
    branch, gate_part = call(
        functools.partial(branch_kernel, n),
        [shape((1, tokens, width), bf16), shape((1, width), f32)],
        (gate_vector, cots[0], *parts),
    )
    branch = lax.ppermute(
        branch, both, [(a * n + b, b * n + a) for a in range(n) for b in range(n)]
    )
    gates = [
        lax.ppermute(
            gate_part, both, [(a * n + b, (b ^ k) * n + a) for a in range(n) for b in range(n)]
        )
        for k in range(n)
    ]
    grad_gate = (gates[0] + gates[1]) + (gates[2] + gates[3])
    grad_query, grad_key, grad_value = call(
        functools.partial(unpack_kernel, n),
        [shape((1, tokens, width), bf16)] * 3,
        tuple(outs),
    )
    return (branch, grad_query, grad_key, grad_value, grad_weight, grad_gate)


def solution(mesh):
    placed = (
        P("dp", "seq", "tensor"),
        P("dp", "seq", "tensor"),
        P("dp", "seq", "tensor"),
        P("dp"),
        P("seq", "tensor"),
        P("dp", None),
        P("dp", "seq", "tensor"),
    )
    n = mesh.shape["seq"]

    def body(query_rows, *rest):
        tokens, width = query_rows.shape[1:]
        square = (
            n == 4
            and mesh.shape["tensor"] == n
            and mesh.shape["dp"] == 2
            and width == (n + n // 2) * HD
            and tokens % 64 == 0
        )
        if square:
            return square_shards(n, query_rows, *rest)
        return general_shards(query_rows, *rest)

    return jax.shard_map(
        body,
        mesh=mesh,
        in_specs=placed,
        out_specs=(
            P("dp", "seq", "tensor"),
            P("dp", "seq", "tensor"),
            P("dp", "seq", "tensor"),
            P("dp", "seq", "tensor"),
            P("seq", "tensor"),
            P("dp", "tensor"),
        ),
        check_vma=False,
    )
```

```python
import functools
import math

import jax
import jax.numpy as jnp
from jax import lax
from jax.experimental import pallas as pl
from jax.experimental.pallas import tpu as pltpu
from jax.sharding import PartitionSpec as P

HD = 128


MASKED_SCORE = -1e30


def block_rows(piece_rows):
    return math.gcd(piece_rows, 512)


def query_terms(
    query_heads, grad_heads, row_lse, row_delta, key_block, value_block, key_live, score_scale
):
    scores = (
        jnp.einsum("thd,shd->ths", query_heads, key_block, preferred_element_type=jnp.float32)
        * score_scale
    )
    probs = jnp.where(key_live[None, None, :], jnp.exp(scores - row_lse[:, :, None]), 0.0)
    grad_probs = jnp.einsum(
        "thd,shd->ths", grad_heads, value_block, preferred_element_type=jnp.float32
    )
    dscores = (probs * (grad_probs - row_delta[:, :, None]) * score_scale).astype(jnp.bfloat16)
    return jnp.einsum("ths,shd->thd", dscores, key_block, preferred_element_type=jnp.float32)


def key_terms(
    query_block, grad_block, lse_block, delta_block, key_heads, value_heads, key_live, score_scale
):
    scores = (
        jnp.einsum("shd,thd->sht", query_block, key_heads, preferred_element_type=jnp.float32)
        * score_scale
    )
    probs = jnp.where(key_live[None, None, :], jnp.exp(scores - lse_block[:, :, None]), 0.0)
    value_part = jnp.einsum(
        "sht,shd->thd", probs.astype(jnp.bfloat16), grad_block, preferred_element_type=jnp.float32
    )
    grad_probs = jnp.einsum(
        "shd,thd->sht", grad_block, value_heads, preferred_element_type=jnp.float32
    )
    dscores = (probs * (grad_probs - delta_block[:, :, None]) * score_scale).astype(jnp.bfloat16)
    key_part = jnp.einsum("sht,shd->thd", dscores, query_block, preferred_element_type=jnp.float32)
    return (key_part, value_part)


def general_shards(query_rows, key_rows, value_rows, lengths, out_weight, gate_vector, cotangent):
    tokens = query_rows.shape[1]
    local_width = query_rows.shape[2]
    head_count = local_width // HD
    score_scale = 1.0 / math.sqrt(HD)
    length = lengths[0]
    query_local = query_rows[0]
    key_local = key_rows[0]
    value_local = value_rows[0]
    query_heads = query_local.reshape(tokens, head_count, HD)
    key_heads = key_local.reshape(tokens, head_count, HD)
    value_heads = value_local.reshape(tokens, head_count, HD)
    head_zeros = jnp.zeros((tokens, head_count, HD), jnp.float32)
    start_top = jnp.full((tokens, head_count), MASKED_SCORE, jnp.float32)
    start_total = jnp.zeros((tokens, head_count), jnp.float32)
    key_piece = lax.all_gather(key_local, "seq", axis=0, tiled=True)
    value_piece = lax.all_gather(value_local, "seq", axis=0, tiled=True)
    piece_rows = key_piece.shape[0]
    step_rows = block_rows(piece_rows)

    def forward_block_step(block_index, state):
        row_top, row_total, summed = state
        offset = block_index * step_rows
        key_block = lax.dynamic_slice_in_dim(key_piece, offset, step_rows, 0).reshape(
            step_rows, head_count, HD
        )
        value_block = lax.dynamic_slice_in_dim(value_piece, offset, step_rows, 0).reshape(
            step_rows, head_count, HD
        )
        key_live = offset + jnp.arange(step_rows) < length
        scores = (
            jnp.einsum("thd,shd->ths", query_heads, key_block, preferred_element_type=jnp.float32)
            * score_scale
        )
        masked = jnp.where(key_live[None, None, :], scores, MASKED_SCORE)
        new_top = jnp.maximum(row_top, jnp.max(masked, axis=2))
        weights = jnp.where(key_live[None, None, :], jnp.exp(masked - new_top[:, :, None]), 0.0)
        shrink = jnp.exp(row_top - new_top)
        row_total = row_total * shrink + jnp.sum(weights, axis=2)
        summed = summed * shrink[:, :, None] + jnp.einsum(
            "ths,shd->thd",
            weights.astype(jnp.bfloat16),
            value_block,
            preferred_element_type=jnp.float32,
        )
        return (new_top, row_total, summed)

    row_top, row_total, summed = lax.fori_loop(
        0, piece_rows // step_rows, forward_block_step, (start_top, start_total, head_zeros)
    )
    attended_heads = (summed / row_total[:, :, None]).astype(jnp.bfloat16)
    attended = attended_heads.reshape(tokens, local_width)
    row_lse = row_top + jnp.log(row_total)
    weight_whole = lax.all_gather(out_weight, "seq", axis=0, tiled=True)
    partial_value = jnp.einsum(
        "tk,rk->tr", attended, weight_whole, preferred_element_type=jnp.float32
    )
    projected = lax.psum_scatter(
        partial_value.astype(jnp.bfloat16), "tensor", scatter_dimension=1, tiled=True
    ).astype(jnp.float32)
    out_width = projected.shape[1]
    gate_local = lax.dynamic_slice_in_dim(
        gate_vector[0], lax.axis_index("tensor") * out_width, out_width
    )
    cot_rows = cotangent[0].astype(jnp.float32)
    branch = (gate_local[None, :] * projected).astype(jnp.bfloat16)
    gate_grad = lax.psum(jnp.sum(cot_rows * projected, axis=0), "seq")
    grad_proj = (gate_local[None, :] * cot_rows).astype(jnp.bfloat16)
    grad_full = lax.all_gather(grad_proj, "tensor", axis=1, tiled=True)
    grad_att = jnp.dot(grad_full, weight_whole, preferred_element_type=jnp.float32).astype(
        jnp.bfloat16
    )
    row_share = lax.psum_scatter(
        jnp.einsum("tr,tk->rk", grad_full, attended, preferred_element_type=jnp.float32).astype(
            jnp.bfloat16
        ),
        "seq",
        scatter_dimension=0,
        tiled=True,
    )
    grad_weight = lax.psum(row_share, "dp").astype(jnp.float32)
    grad_heads = grad_att.reshape(tokens, head_count, HD)
    row_delta = jnp.sum(grad_heads.astype(jnp.float32) * attended_heads.astype(jnp.float32), axis=2)
    all_lse, all_delta = (
        lax.all_gather(row_lse, "seq", axis=0, tiled=True),
        lax.all_gather(row_delta, "seq", axis=0, tiled=True),
    )
    key_offset = lax.axis_index("seq") * tokens
    local_live = key_offset + jnp.arange(tokens) < length
    query_key_piece = lax.all_gather(key_local, "seq", axis=0, tiled=True)
    query_value_piece = lax.all_gather(value_local, "seq", axis=0, tiled=True)
    piece_rows = query_key_piece.shape[0]
    query_step_rows = block_rows(piece_rows)

    def query_block_step(block_index, state):
        offset = block_index * query_step_rows
        key_block = lax.dynamic_slice_in_dim(query_key_piece, offset, query_step_rows, 0).reshape(
            query_step_rows, head_count, HD
        )
        value_block = lax.dynamic_slice_in_dim(
            query_value_piece, offset, query_step_rows, 0
        ).reshape(query_step_rows, head_count, HD)
        key_live = offset + jnp.arange(query_step_rows) < length
        return state + query_terms(
            query_heads,
            grad_heads,
            row_lse,
            row_delta,
            key_block,
            value_block,
            key_live,
            score_scale,
        )

    grad_q = lax.fori_loop(0, piece_rows // query_step_rows, query_block_step, head_zeros)
    query_piece = lax.all_gather(query_local, "seq", axis=0, tiled=True)
    grad_piece = lax.all_gather(grad_att, "seq", axis=0, tiled=True)
    piece_rows = query_piece.shape[0]
    key_step_rows = block_rows(piece_rows)

    def key_block_step(block_index, state):
        offset = block_index * key_step_rows
        query_block = lax.dynamic_slice_in_dim(query_piece, offset, key_step_rows, 0).reshape(
            key_step_rows, head_count, HD
        )
        grad_block = lax.dynamic_slice_in_dim(grad_piece, offset, key_step_rows, 0).reshape(
            key_step_rows, head_count, HD
        )
        lse_block = lax.dynamic_slice_in_dim(all_lse, offset, key_step_rows, 0)
        delta_block = lax.dynamic_slice_in_dim(all_delta, offset, key_step_rows, 0)
        key_part, value_part = key_terms(
            query_block,
            grad_block,
            lse_block,
            delta_block,
            key_heads,
            value_heads,
            local_live,
            score_scale,
        )
        return (state[0] + key_part, state[1] + value_part)

    grad_k, grad_v = lax.fori_loop(
        0, piece_rows // key_step_rows, key_block_step, (head_zeros, head_zeros)
    )
    grad_query = grad_q.reshape(tokens, local_width).astype(jnp.bfloat16)
    grad_key = grad_k.reshape(tokens, local_width).astype(jnp.bfloat16)
    grad_value = grad_v.reshape(tokens, local_width).astype(jnp.bfloat16)
    return (
        branch[None],
        grad_query[None],
        grad_key[None],
        grad_value[None],
        grad_weight,
        gate_grad[None],
    )


VMEM_LIMIT = 40 * 1024 * 1024
NT = (((1,), (1,)), ((), ()))
TN = (((0,), (0,)), ((), ()))
NN = (((1,), (0,)), ((), ()))


def mm(left, right, dims):
    return lax.dot_general(left, right, dims, preferred_element_type=jnp.float32)


def lane_block(index, width):
    return pl.ds(pl.multiple_of(index * width, HD), width)


def call(kernel, out_shape, args, flops=0, smem=(), scratch=(), space=pltpu.VMEM, out_space=pltpu.VMEM, limit=VMEM_LIMIT):
    nbytes = sum(a.size * a.dtype.itemsize for a in args)
    nbytes += sum(math.prod(o.shape) * o.dtype.itemsize for o in jax.tree.leaves(out_shape))
    return pl.pallas_call(
        kernel,
        out_shape=out_shape,
        in_specs=[
            pl.BlockSpec(memory_space=pltpu.SMEM if i in smem else space)
            for i in range(len(args))
        ],
        out_specs=jax.tree.map(lambda _: pl.BlockSpec(memory_space=out_space), out_shape),
        scratch_shapes=list(scratch),
        compiler_params=pltpu.CompilerParams(vmem_limit_bytes=limit),
        cost_estimate=pl.CostEstimate(flops=flops, bytes_accessed=nbytes, transcendentals=0),
    )(*args)


def xor_pairs(count, k):
    return [(i, i ^ k) for i in range(count)]


def pack_kernel(q_ref, k_ref, v_ref, w_ref, kv_ref, q_own_ref, send_ref, near_ref, near2_ref, sems):
    s, core = lax.axis_index("seq"), lax.axis_index("dp")
    width, quarter = q_own_ref.shape[1], near_ref.shape[0]
    own, other = lane_block(s % 2, width), lane_block(1 - s % 2, width)
    pairs = [
        (k_ref.at[0, :, other], send_ref.at[0]),
        (v_ref.at[0, :, other], send_ref.at[1]),
        (q_ref.at[0, :, other], send_ref.at[2]),
        (k_ref.at[0, :, own], kv_ref.at[0]),
        (v_ref.at[0, :, own], kv_ref.at[1]),
        (q_ref.at[0, :, own], q_own_ref),
    ]
    for i, ref in enumerate((near_ref, near2_ref)):
        at = pl.multiple_of((2 * core + i) * quarter, quarter)
        pairs.append((w_ref.at[pl.ds(at, quarter), :], ref))
    copies = [pltpu.make_async_copy(a, b, sems.at[i]) for i, (a, b) in enumerate(pairs)]
    for copy in copies:
        copy.start()
    for copy in copies:
        copy.wait()


def head_rows(parts, head):
    return jnp.concatenate([p[:, head * HD : (head + 1) * HD] for p in parts], axis=0)


def live_bias(s, n, rows, length):
    parts = []
    for k in range(n):
        place = (s ^ k) * rows + lax.broadcasted_iota(jnp.int32, (rows, 1), 0)
        parts.append(jnp.where(place < length, 0.0, MASKED_SCORE))
    return jnp.concatenate(parts, axis=0)


def forward_kernel(n, scale, len_ref, *refs):
    kvs, queries, (o_ref, lse_ref) = refs[:n], (refs[n], refs[1].at[2]), refs[n + 1 :]
    s = lax.axis_index("seq")
    rows = o_ref.shape[1]
    bias = live_bias(s, n, rows, len_ref[0])
    for head in range(o_ref.shape[2] // HD):
        keys = head_rows([kv.at[0] for kv in kvs], head)
        values = head_rows([kv.at[1] for kv in kvs], head)
        scores = mm(keys, head_rows(queries, head), NT) * scale + bias
        top = jnp.max(scores, axis=0, keepdims=True)
        weights = jnp.exp(scores - top)
        total = jnp.sum(weights, axis=0, keepdims=True)
        summed = mm(values, weights.astype(jnp.bfloat16), TN)
        attended = (summed / total).T.astype(jnp.bfloat16)
        lse_ref[head : head + 1, :] = top + jnp.log(total)
        for u in range(2):
            o_ref[u, :, head * HD : (head + 1) * HD] = attended[u * rows : (u + 1) * rows]


def join_quarters(core, own_refs, other_refs, out_ref):
    rows = own_refs[0].shape[0]
    for i in range(2):
        at = pl.multiple_of((2 * core + i) * rows, rows)
        out_ref[pl.ds(at, rows), :] = own_refs[i][...]
        at = pl.multiple_of((2 * (1 - core) + i) * rows, rows)
        out_ref[pl.ds(at, rows), :] = other_refs[i][...]


def grad_attended_kernel(n, gate_ref, w_ref, *refs):
    quarters, cots, (own_ref, send_ref, cot_ref, w2_ref, share_ref) = refs[:4], refs[4 : 4 + n], refs[4 + n :]
    s = lax.axis_index("seq")
    rows, heads_width = own_ref.shape[1:]
    size = w_ref.shape[0]
    t = lax.axis_index("tensor")
    join_quarters(lax.axis_index("dp"), quarters[:2], quarters[2:], w2_ref)
    for k in range(n):
        cot_ref[s ^ t ^ k] = cots[k][0]
    total = None
    for b, weight_ref in ((0, w_ref), (1, w2_ref)):
        gate = gate_ref[:, lane_block(s ^ (2 * b), size)]
        cot = jnp.concatenate([cot_ref[2 * b], cot_ref[2 * b + 1]], axis=0)
        grad_proj = (gate * cot.astype(jnp.float32)).astype(jnp.bfloat16)
        part = mm(grad_proj, weight_ref[...], NN)
        total = part if total is None else total + part
    share_ref[...] = total
    own, other = lane_block(s % 2, heads_width), lane_block(1 - s % 2, heads_width)
    for u in range(2):
        own_ref[u] = share_ref[u * rows : (u + 1) * rows, own]
        send_ref[1 - u] = share_ref[u * rows : (u + 1) * rows, other].astype(jnp.bfloat16)


def backward_kernel(n, scale, len_ref, lse_ref, o_ref, own_ref, other_ref, *refs):
    kvs, queries = refs[:n], (refs[n], refs[1].at[2])
    dq_refs, dkv_refs = refs[n + 1 : n + 3], refs[n + 3 :]
    s = lax.axis_index("seq")
    rows = o_ref.shape[1]
    bias = live_bias(s, n, rows, len_ref[0])
    for head in range(o_ref.shape[2] // HD):
        lanes = slice(head * HD, (head + 1) * HD)
        keys = head_rows([kv.at[0] for kv in kvs], head)
        values = head_rows([kv.at[1] for kv in kvs], head)
        query = head_rows(queries, head)
        grad = jnp.concatenate(
            [own_ref[u, :, lanes] + other_ref[u, :, lanes].astype(jnp.float32) for u in range(2)],
            axis=0,
        ).astype(jnp.bfloat16)
        attended = jnp.concatenate([o_ref[u, :, lanes] for u in range(2)], axis=0)
        product = grad.astype(jnp.float32) * attended.astype(jnp.float32)
        delta = jnp.sum(product.T, axis=0, keepdims=True)
        scores = mm(keys, query, NT) * scale + bias
        probs = jnp.exp(scores - lse_ref[head : head + 1, :])
        grad_probs = mm(values, grad, NT)
        dscores = (probs * (grad_probs - delta) * scale).astype(jnp.bfloat16)
        grad_values = mm(probs.astype(jnp.bfloat16), grad, NN)
        grad_keys = mm(dscores, query, NN)
        grad_query = mm(keys, dscores, TN).T.astype(jnp.bfloat16)
        for u in range(2):
            dq_refs[u][:, lanes] = grad_query[u * rows : (u + 1) * rows]
        for k in range(n):
            out = dkv_refs[k]
            out[0, :, lanes] = grad_keys[k * rows : (k + 1) * rows].astype(out.dtype)
            out[1, :, lanes] = grad_values[k * rows : (k + 1) * rows].astype(out.dtype)


def forward_sum_kernel(own_ref, other_ref, out_ref):
    out_ref[...] = (own_ref[...] + other_ref[...].astype(jnp.float32)).astype(jnp.bfloat16)


def unpack_kernel(dq_ref, dq_other_ref, own_ref, part_ref, other_ref, *outs):
    s = lax.axis_index("seq")
    own, other = lane_block(s % 2, dq_ref.shape[1]), lane_block(1 - s % 2, dq_ref.shape[1])
    outs[0][0, :, own] = dq_ref[...]
    outs[0][0, :, other] = dq_other_ref[...]
    for i in range(2):
        total = own_ref[i] + part_ref[i].astype(jnp.float32)
        outs[1 + i][0, :, own] = total.astype(jnp.bfloat16)
        outs[1 + i][0, :, other] = other_ref[i]


def project_kernel(n, w_ref, w2_ref, o_ref, other_ref, *refs):
    (own_ref, *send_refs), (all_ref, parts_ref) = refs[:n], refs[n:]
    s, t = lax.axis_index("seq"), lax.axis_index("tensor")
    rows, heads_width = o_ref.shape[1:]
    own, other = lane_block(s % 2, heads_width), lane_block(1 - s % 2, heads_width)
    for u in range(2):
        all_ref[u * rows : (u + 1) * rows, own] = o_ref[u]
        all_ref[u * rows : (u + 1) * rows, other] = other_ref[1 - u]
    for b, weight_ref in ((0, w_ref), (1, w2_ref)):
        part = mm(all_ref[...], weight_ref[...], NT)
        for u in range(2):
            parts_ref[2 * b + u] = part[u * rows : (u + 1) * rows]
    own_ref[...] = parts_ref[s ^ t]
    for k in range(1, n):
        send_refs[k - 1][...] = parts_ref[s ^ t ^ k].astype(jnp.bfloat16)


def grad_weight_kernel(gate_ref, all_ref, cot_ref, keep_ref, send_ref, outer_ref):
    core, s = lax.axis_index("dp"), lax.axis_index("seq")
    size = all_ref.shape[1]
    half = size // 2
    for b in range(2):
        gate = gate_ref[:, lane_block(s ^ (2 * b), size)]
        cot = jnp.concatenate([cot_ref[2 * b], cot_ref[2 * b + 1]], axis=0)
        grad_proj = (gate * cot.astype(jnp.float32)).astype(jnp.bfloat16)
        outer_ref[...] = mm(grad_proj, all_ref[...], TN)
        keep_ref[b] = outer_ref[pl.ds(pl.multiple_of(core * half, half), half), :]
        send_ref[b] = outer_ref[pl.ds(pl.multiple_of((1 - core) * half, half), half), :].astype(
            jnp.bfloat16
        )


def weight_clips_kernel(keep_ref, other_ref, own_ref, send_ref):
    own_ref[...] = keep_ref[0] + other_ref[0].astype(jnp.float32)
    send_ref[...] = (keep_ref[1] + other_ref[1].astype(jnp.float32)).astype(jnp.bfloat16)


def weight_halves_kernel(own_ref, other_ref, out_ref):
    out_ref[...] = (own_ref[...] + other_ref[...].astype(jnp.float32)).astype(jnp.bfloat16)


def weight_join_kernel(own_ref, other_ref, out_ref):
    core = lax.axis_index("dp")
    half = own_ref.shape[0]
    own = pl.ds(pl.multiple_of(core * half, half), half)
    out_ref[own, :] = own_ref[...].astype(jnp.float32)
    other = pl.ds(pl.multiple_of((1 - core) * half, half), half)
    out_ref[other, :] = other_ref[...].astype(jnp.float32)


def projected_kernel(n, own_ref, *refs):
    parts, out_ref = refs[: n - 1], refs[n - 1]
    projected = own_ref[...]
    for part in parts:
        projected = projected + part[...].astype(jnp.float32)
    out_ref[...] = projected.astype(jnp.bfloat16)


def branch_kernel(gate_ref, cot_ref, projected_ref, branch_ref, gate_grad_ref):
    projected = projected_ref[...].astype(jnp.float32)
    gate = gate_ref[:, lane_block(lax.axis_index("tensor"), projected.shape[1])]
    branch_ref[0] = (gate * projected).astype(jnp.bfloat16)
    cot = cot_ref[0].astype(jnp.float32)
    gate_grad_ref[...] = jnp.sum(cot * projected, axis=0, keepdims=True)


def square_shards(
    n, query_rows, key_rows, value_rows, lengths, out_weight, gate_vector, cotangent
):
    tokens, width = query_rows.shape[1:]
    scale = 1.0 / math.sqrt(HD)
    bf16, f32 = jnp.bfloat16, jnp.float32
    shape = jax.ShapeDtypeStruct
    both = ("seq", "tensor")
    both_pairs = [(a, b) for a in range(n) for b in range(n)]

    def permute(value, axes, k):
        return lax.ppermute(value, axes, xor_pairs(n, k))

    def swap(value):
        return lax.ppermute(value, "dp", xor_pairs(2, 1))

    width_half = width // 2
    rows_kv, rows_q = (2, tokens, width_half), (tokens, width_half)
    kv, query, send, near_a, near_b = call(
        pack_kernel,
        [
            shape(rows_kv, bf16),
            shape(rows_q, bf16),
            shape((3, tokens, width_half), bf16),
            *[shape((width_half // 2, width), bf16)] * 2,
        ],
        (query_rows, key_rows, value_rows, out_weight),
        scratch=[pltpu.SemaphoreType.DMA((8,))],
        space=pl.ANY,
        limit=60 * 1024 * 1024,
    )

    def turn(value, k):
        return lax.ppermute(
            value,
            both,
            [
                (a * n + b, ((a & 2) | (b & 1)) * n + (b ^ k ^ ((a ^ b) & 1)))
                for a, b in both_pairs
            ],
        )

    qkv_x, kv_y, near_a, cot_1, cot_2, near_b, cot_late = lax.optimization_barrier(
        (
            permute(send, "seq", 1),
            permute(kv, "seq", 2),
            permute(near_a, "seq", 2),
            turn(cotangent, 1),
            turn(cotangent, 2),
            near_b,
            cotangent,
        )
    )
    kv_xy, near_b, cot_0, cot_3, far_a, qkv_x, kv_y, query = lax.optimization_barrier(
        (
            permute(qkv_x[:2], "seq", 2),
            permute(near_b, "seq", 2),
            turn(cot_late, 0),
            turn(cot_late, 3),
            swap(near_a),
            qkv_x,
            kv_y,
            query,
        )
    )
    cots = (cot_0, cot_1, cot_2, cot_3)
    kvs = (kv, qkv_x, kv_y, kv_xy)
    block = 2 * tokens
    unit_flops = 2 * n * tokens * block * HD
    wide_flops = 4 * block * width * width
    attended, lse = call(
        functools.partial(forward_kernel, n, scale),
        [shape(rows_kv, bf16), shape((width_half // HD, block), f32)],
        (lengths, *kvs, query),
        flops=6 * unit_flops,
        smem=(0,),
    )
    heads = (attended, permute(attended, "seq", 1))
    grad_own, grad_send, cot_all, weight_y = call(
        functools.partial(grad_attended_kernel, n),
        [
            shape(rows_kv, f32),
            shape(rows_kv, bf16),
            shape((n, tokens, width), bf16),
            shape((width, width), bf16),
        ],
        (gate_vector, out_weight, near_a, near_b, far_a, swap(near_b), *cots),
        flops=wide_flops,
        scratch=[pltpu.VMEM((block, width), f32)],
    )
    grad_other = permute(grad_send, "seq", 1)
    *parts, attended_all = call(
        functools.partial(project_kernel, n),
        [
            shape((tokens, width), f32),
            *[shape((tokens, width), bf16)] * (n - 1),
            shape((block, width), bf16),
        ],
        (out_weight, weight_y, *heads),
        flops=wide_flops,
        scratch=[pltpu.VMEM((n, tokens, width), f32)],
    )
    dq, dq_send, dkv, dkv_x, dkv_y, dkv_xy = call(
        functools.partial(backward_kernel, n, scale),
        [shape(rows_q, bf16)] * 2 + [shape(rows_kv, f32)] * 2 + [shape(rows_kv, bf16)] * 2,
        (lengths, lse, attended, grad_own, grad_other, *kvs, query),
        flops=15 * unit_flops,
        smem=(0,),
    )
    keep, send = call(
        grad_weight_kernel,
        [shape((2, width_half, width), f32), shape((2, width_half, width), bf16)],
        (gate_vector, attended_all, cot_all),
        flops=wide_flops,
        scratch=[pltpu.VMEM((width, width), f32)],
    )
    parts = [parts[0]] + [permute(parts[k], "tensor", k) for k in range(1, n)]
    own, send = call(
        weight_clips_kernel,
        [shape((width_half, width), f32), shape((width_half, width), bf16)],
        (keep, swap(send)),
    )
    fin = call(
        weight_halves_kernel, shape((width_half, width), bf16), (own, permute(send, "seq", 2))
    )
    grad_weight = call(weight_join_kernel, shape((width, width), f32), (fin, swap(fin)))
    dq_other, dkv_xy = permute(dq_send, "seq", 1), permute(dkv_xy, "seq", 2)
    dkv_y = permute(dkv_y, "seq", 2)
    dkv_xy, dq_other = lax.optimization_barrier((dkv_xy, dq_other))
    dkv_x = call(forward_sum_kernel, shape(rows_kv, bf16), (dkv_x, dkv_xy))
    dkv_other = permute(dkv_x, "seq", 1)
    projected = call(
        functools.partial(projected_kernel, n), shape((tokens, width), bf16), tuple(parts)
    )
    home = [(a * n + b, (a ^ 1) * n + (b ^ 1) if (a ^ b) & 1 else a * n + b) for a, b in both_pairs]
    projected = lax.ppermute(projected, both, home)
    branch, grad_gate = call(
        branch_kernel,
        [shape((1, tokens, width), bf16), shape((1, width), f32)],
        (gate_vector, cotangent, projected),
    )
    for k in (1, 2):
        grad_gate = grad_gate + permute(grad_gate, "seq", k)
    grad_query, grad_key, grad_value = call(
        unpack_kernel,
        [shape((1, tokens, width), bf16)] * 3,
        (dq, dq_other, dkv, dkv_y, dkv_other),
    )
    return (branch, grad_query, grad_key, grad_value, grad_weight, grad_gate)


def solution(mesh):
    placed = (
        P("dp", "seq", "tensor"),
        P("dp", "seq", "tensor"),
        P("dp", "seq", "tensor"),
        P("dp"),
        P("seq", "tensor"),
        P("dp", None),
        P("dp", "seq", "tensor"),
    )
    n = mesh.shape["seq"]

    def body(query_rows, *rest):
        tokens, width = query_rows.shape[1:]
        square = (
            n == 4
            and mesh.shape["tensor"] == n
            and mesh.shape["dp"] == 2
            and width % (2 * HD) == 0
            and tokens % 32 == 0
        )
        if square:
            return square_shards(n, query_rows, *rest)
        return general_shards(query_rows, *rest)

    return jax.shard_map(
        body,
        mesh=mesh,
        in_specs=placed,
        out_specs=(
            P("dp", "seq", "tensor"),
            P("dp", "seq", "tensor"),
            P("dp", "seq", "tensor"),
            P("dp", "seq", "tensor"),
            P("seq", "tensor"),
            P("dp", "tensor"),
        ),
        check_vma=False,
    )
```

```python
import functools
import math

import jax
import jax.numpy as jnp
from jax import lax
from jax.experimental import pallas as pl
from jax.experimental.pallas import tpu as pltpu
from jax.sharding import PartitionSpec as P

HD = 128


MASKED_SCORE = -1e30


def block_rows(piece_rows):
    return math.gcd(piece_rows, 512)


def query_terms(
    query_heads, grad_heads, row_lse, row_delta, key_block, value_block, key_live, score_scale
):
    scores = (
        jnp.einsum("thd,shd->ths", query_heads, key_block, preferred_element_type=jnp.float32)
        * score_scale
    )
    probs = jnp.where(key_live[None, None, :], jnp.exp(scores - row_lse[:, :, None]), 0.0)
    grad_probs = jnp.einsum(
        "thd,shd->ths", grad_heads, value_block, preferred_element_type=jnp.float32
    )
    dscores = (probs * (grad_probs - row_delta[:, :, None]) * score_scale).astype(jnp.bfloat16)
    return jnp.einsum("ths,shd->thd", dscores, key_block, preferred_element_type=jnp.float32)


def key_terms(
    query_block, grad_block, lse_block, delta_block, key_heads, value_heads, key_live, score_scale
):
    scores = (
        jnp.einsum("shd,thd->sht", query_block, key_heads, preferred_element_type=jnp.float32)
        * score_scale
    )
    probs = jnp.where(key_live[None, None, :], jnp.exp(scores - lse_block[:, :, None]), 0.0)
    value_part = jnp.einsum(
        "sht,shd->thd", probs.astype(jnp.bfloat16), grad_block, preferred_element_type=jnp.float32
    )
    grad_probs = jnp.einsum(
        "shd,thd->sht", grad_block, value_heads, preferred_element_type=jnp.float32
    )
    dscores = (probs * (grad_probs - delta_block[:, :, None]) * score_scale).astype(jnp.bfloat16)
    key_part = jnp.einsum("sht,shd->thd", dscores, query_block, preferred_element_type=jnp.float32)
    return (key_part, value_part)


def general_shards(query_rows, key_rows, value_rows, lengths, out_weight, gate_vector, cotangent):
    tokens = query_rows.shape[1]
    local_width = query_rows.shape[2]
    head_count = local_width // HD
    score_scale = 1.0 / math.sqrt(HD)
    length = lengths[0]
    query_local = query_rows[0]
    key_local = key_rows[0]
    value_local = value_rows[0]
    query_heads = query_local.reshape(tokens, head_count, HD)
    key_heads = key_local.reshape(tokens, head_count, HD)
    value_heads = value_local.reshape(tokens, head_count, HD)
    head_zeros = jnp.zeros((tokens, head_count, HD), jnp.float32)
    start_top = jnp.full((tokens, head_count), MASKED_SCORE, jnp.float32)
    start_total = jnp.zeros((tokens, head_count), jnp.float32)
    key_piece = lax.all_gather(key_local, "seq", axis=0, tiled=True)
    value_piece = lax.all_gather(value_local, "seq", axis=0, tiled=True)
    piece_rows = key_piece.shape[0]
    step_rows = block_rows(piece_rows)

    def forward_block_step(block_index, state):
        row_top, row_total, summed = state
        offset = block_index * step_rows
        key_block = lax.dynamic_slice_in_dim(key_piece, offset, step_rows, 0).reshape(
            step_rows, head_count, HD
        )
        value_block = lax.dynamic_slice_in_dim(value_piece, offset, step_rows, 0).reshape(
            step_rows, head_count, HD
        )
        key_live = offset + jnp.arange(step_rows) < length
        scores = (
            jnp.einsum("thd,shd->ths", query_heads, key_block, preferred_element_type=jnp.float32)
            * score_scale
        )
        masked = jnp.where(key_live[None, None, :], scores, MASKED_SCORE)
        new_top = jnp.maximum(row_top, jnp.max(masked, axis=2))
        weights = jnp.where(key_live[None, None, :], jnp.exp(masked - new_top[:, :, None]), 0.0)
        shrink = jnp.exp(row_top - new_top)
        row_total = row_total * shrink + jnp.sum(weights, axis=2)
        summed = summed * shrink[:, :, None] + jnp.einsum(
            "ths,shd->thd",
            weights.astype(jnp.bfloat16),
            value_block,
            preferred_element_type=jnp.float32,
        )
        return (new_top, row_total, summed)

    row_top, row_total, summed = lax.fori_loop(
        0, piece_rows // step_rows, forward_block_step, (start_top, start_total, head_zeros)
    )
    attended_heads = (summed / row_total[:, :, None]).astype(jnp.bfloat16)
    attended = attended_heads.reshape(tokens, local_width)
    row_lse = row_top + jnp.log(row_total)
    weight_whole = lax.all_gather(out_weight, "seq", axis=0, tiled=True)
    partial_value = jnp.einsum(
        "tk,rk->tr", attended, weight_whole, preferred_element_type=jnp.float32
    )
    projected = lax.psum_scatter(
        partial_value.astype(jnp.bfloat16), "tensor", scatter_dimension=1, tiled=True
    ).astype(jnp.float32)
    out_width = projected.shape[1]
    gate_local = lax.dynamic_slice_in_dim(
        gate_vector[0], lax.axis_index("tensor") * out_width, out_width
    )
    cot_rows = cotangent[0].astype(jnp.float32)
    branch = (gate_local[None, :] * projected).astype(jnp.bfloat16)
    gate_grad = lax.psum(jnp.sum(cot_rows * projected, axis=0), "seq")
    grad_proj = (gate_local[None, :] * cot_rows).astype(jnp.bfloat16)
    grad_full = lax.all_gather(grad_proj, "tensor", axis=1, tiled=True)
    grad_att = jnp.dot(grad_full, weight_whole, preferred_element_type=jnp.float32).astype(
        jnp.bfloat16
    )
    row_share = lax.psum_scatter(
        jnp.einsum("tr,tk->rk", grad_full, attended, preferred_element_type=jnp.float32).astype(
            jnp.bfloat16
        ),
        "seq",
        scatter_dimension=0,
        tiled=True,
    )
    grad_weight = lax.psum(row_share, "dp").astype(jnp.float32)
    grad_heads = grad_att.reshape(tokens, head_count, HD)
    row_delta = jnp.sum(grad_heads.astype(jnp.float32) * attended_heads.astype(jnp.float32), axis=2)
    all_lse, all_delta = (
        lax.all_gather(row_lse, "seq", axis=0, tiled=True),
        lax.all_gather(row_delta, "seq", axis=0, tiled=True),
    )
    key_offset = lax.axis_index("seq") * tokens
    local_live = key_offset + jnp.arange(tokens) < length
    query_key_piece = lax.all_gather(key_local, "seq", axis=0, tiled=True)
    query_value_piece = lax.all_gather(value_local, "seq", axis=0, tiled=True)
    piece_rows = query_key_piece.shape[0]
    query_step_rows = block_rows(piece_rows)

    def query_block_step(block_index, state):
        offset = block_index * query_step_rows
        key_block = lax.dynamic_slice_in_dim(query_key_piece, offset, query_step_rows, 0).reshape(
            query_step_rows, head_count, HD
        )
        value_block = lax.dynamic_slice_in_dim(
            query_value_piece, offset, query_step_rows, 0
        ).reshape(query_step_rows, head_count, HD)
        key_live = offset + jnp.arange(query_step_rows) < length
        return state + query_terms(
            query_heads,
            grad_heads,
            row_lse,
            row_delta,
            key_block,
            value_block,
            key_live,
            score_scale,
        )

    grad_q = lax.fori_loop(0, piece_rows // query_step_rows, query_block_step, head_zeros)
    query_piece = lax.all_gather(query_local, "seq", axis=0, tiled=True)
    grad_piece = lax.all_gather(grad_att, "seq", axis=0, tiled=True)
    piece_rows = query_piece.shape[0]
    key_step_rows = block_rows(piece_rows)

    def key_block_step(block_index, state):
        offset = block_index * key_step_rows
        query_block = lax.dynamic_slice_in_dim(query_piece, offset, key_step_rows, 0).reshape(
            key_step_rows, head_count, HD
        )
        grad_block = lax.dynamic_slice_in_dim(grad_piece, offset, key_step_rows, 0).reshape(
            key_step_rows, head_count, HD
        )
        lse_block = lax.dynamic_slice_in_dim(all_lse, offset, key_step_rows, 0)
        delta_block = lax.dynamic_slice_in_dim(all_delta, offset, key_step_rows, 0)
        key_part, value_part = key_terms(
            query_block,
            grad_block,
            lse_block,
            delta_block,
            key_heads,
            value_heads,
            local_live,
            score_scale,
        )
        return (state[0] + key_part, state[1] + value_part)

    grad_k, grad_v = lax.fori_loop(
        0, piece_rows // key_step_rows, key_block_step, (head_zeros, head_zeros)
    )
    grad_query = grad_q.reshape(tokens, local_width).astype(jnp.bfloat16)
    grad_key = grad_k.reshape(tokens, local_width).astype(jnp.bfloat16)
    grad_value = grad_v.reshape(tokens, local_width).astype(jnp.bfloat16)
    return (
        branch[None],
        grad_query[None],
        grad_key[None],
        grad_value[None],
        grad_weight,
        gate_grad[None],
    )


VMEM_LIMIT = 40 * 1024 * 1024
NT = (((1,), (1,)), ((), ()))
TN = (((0,), (0,)), ((), ()))
NN = (((1,), (0,)), ((), ()))


def mm(left, right, dims):
    return lax.dot_general(left, right, dims, preferred_element_type=jnp.float32)


def lane_block(index, width):
    return pl.ds(pl.multiple_of(index * width, HD), width)


def call(kernel, out_shape, args, flops=0, smem=(), scratch=(), space=pltpu.VMEM, out_space=pltpu.VMEM, limit=VMEM_LIMIT):
    nbytes = sum(a.size * a.dtype.itemsize for a in args)
    nbytes += sum(math.prod(o.shape) * o.dtype.itemsize for o in jax.tree.leaves(out_shape))
    return pl.pallas_call(
        kernel,
        out_shape=out_shape,
        in_specs=[
            pl.BlockSpec(memory_space=pltpu.SMEM if i in smem else space)
            for i in range(len(args))
        ],
        out_specs=jax.tree.map(lambda _: pl.BlockSpec(memory_space=out_space), out_shape),
        scratch_shapes=list(scratch),
        compiler_params=pltpu.CompilerParams(vmem_limit_bytes=limit),
        cost_estimate=pl.CostEstimate(flops=flops, bytes_accessed=nbytes, transcendentals=0),
    )(*args)


def xor_pairs(count, k):
    return [(i, i ^ k) for i in range(count)]


def pack_kernel(q_ref, k_ref, v_ref, w_ref, kv_ref, q_own_ref, send_ref, near_ref, near2_ref, sems):
    s, core = lax.axis_index("seq"), lax.axis_index("dp")
    width, quarter = q_own_ref.shape[1], near_ref.shape[0]
    own, other = lane_block(s % 2, width), lane_block(1 - s % 2, width)
    pairs = [
        (k_ref.at[0, :, other], send_ref.at[0]),
        (v_ref.at[0, :, other], send_ref.at[1]),
        (q_ref.at[0, :, other], send_ref.at[2]),
        (k_ref.at[0, :, own], kv_ref.at[0]),
        (v_ref.at[0, :, own], kv_ref.at[1]),
        (q_ref.at[0, :, own], q_own_ref),
    ]
    for i, ref in enumerate((near_ref, near2_ref)):
        at = pl.multiple_of((2 * core + i) * quarter, quarter)
        pairs.append((w_ref.at[pl.ds(at, quarter), :], ref))
    copies = [pltpu.make_async_copy(a, b, sems.at[i]) for i, (a, b) in enumerate(pairs)]
    for copy in copies:
        copy.start()
    for copy in copies:
        copy.wait()


def head_rows(parts, head):
    return jnp.concatenate([p[:, head * HD : (head + 1) * HD] for p in parts], axis=0)


def live_bias(s, n, rows, length):
    parts = []
    for k in range(n):
        place = (s ^ k) * rows + lax.broadcasted_iota(jnp.int32, (rows, 1), 0)
        parts.append(jnp.where(place < length, 0.0, MASKED_SCORE))
    return jnp.concatenate(parts, axis=0)


def forward_kernel(n, scale, len_ref, *refs):
    kvs, queries, (o_ref, lse_ref) = refs[:n], (refs[n], refs[1].at[2]), refs[n + 1 :]
    s = lax.axis_index("seq")
    rows = o_ref.shape[1]
    bias = live_bias(s, n, rows, len_ref[0])
    for head in range(o_ref.shape[2] // HD):
        keys = head_rows([kv.at[0] for kv in kvs], head)
        values = head_rows([kv.at[1] for kv in kvs], head)
        scores = mm(keys, head_rows(queries, head), NT) * scale + bias
        top = jnp.max(scores, axis=0, keepdims=True)
        weights = jnp.exp(scores - top)
        total = jnp.sum(weights, axis=0, keepdims=True)
        summed = mm(values, weights.astype(jnp.bfloat16), TN)
        attended = (summed / total).T.astype(jnp.bfloat16)
        lse_ref[head : head + 1, :] = top + jnp.log(total)
        for u in range(2):
            o_ref[u, :, head * HD : (head + 1) * HD] = attended[u * rows : (u + 1) * rows]


def join_quarters(core, own_refs, other_refs, out_ref):
    rows = own_refs[0].shape[0]
    for i in range(2):
        at = pl.multiple_of((2 * core + i) * rows, rows)
        out_ref[pl.ds(at, rows), :] = own_refs[i][...]
        at = pl.multiple_of((2 * (1 - core) + i) * rows, rows)
        out_ref[pl.ds(at, rows), :] = other_refs[i][...]


def grad_attended_kernel(n, gate_ref, w_ref, *refs):
    quarters, cots, (own_ref, send_ref, cot_ref, w2_ref, share_ref) = refs[:4], refs[4 : 4 + n], refs[4 + n :]
    s = lax.axis_index("seq")
    rows, heads_width = own_ref.shape[1:]
    size = w_ref.shape[0]
    t = lax.axis_index("tensor")
    join_quarters(lax.axis_index("dp"), quarters[:2], quarters[2:], w2_ref)
    for k in range(n):
        cot_ref[s ^ t ^ k] = cots[k][0]
    total = None
    for b, weight_ref in ((0, w_ref), (1, w2_ref)):
        gate = gate_ref[:, lane_block(s ^ (2 * b), size)]
        cot = jnp.concatenate([cot_ref[2 * b], cot_ref[2 * b + 1]], axis=0)
        grad_proj = (gate * cot.astype(jnp.float32)).astype(jnp.bfloat16)
        part = mm(grad_proj, weight_ref[...], NN)
        total = part if total is None else total + part
    share_ref[...] = total
    own, other = lane_block(s % 2, heads_width), lane_block(1 - s % 2, heads_width)
    for u in range(2):
        own_ref[u] = share_ref[u * rows : (u + 1) * rows, own]
        send_ref[1 - u] = share_ref[u * rows : (u + 1) * rows, other].astype(jnp.bfloat16)


def backward_kernel(n, scale, len_ref, lse_ref, o_ref, own_ref, other_ref, *refs):
    kvs, queries = refs[:n], (refs[n], refs[1].at[2])
    dq_refs, dkv_refs = refs[n + 1 : n + 3], refs[n + 3 :]
    s = lax.axis_index("seq")
    rows = o_ref.shape[1]
    bias = live_bias(s, n, rows, len_ref[0])
    for head in range(o_ref.shape[2] // HD):
        lanes = slice(head * HD, (head + 1) * HD)
        keys = head_rows([kv.at[0] for kv in kvs], head)
        values = head_rows([kv.at[1] for kv in kvs], head)
        query = head_rows(queries, head)
        grad = jnp.concatenate(
            [own_ref[u, :, lanes] + other_ref[u, :, lanes].astype(jnp.float32) for u in range(2)],
            axis=0,
        ).astype(jnp.bfloat16)
        attended = jnp.concatenate([o_ref[u, :, lanes] for u in range(2)], axis=0)
        product = grad.astype(jnp.float32) * attended.astype(jnp.float32)
        delta = jnp.sum(product.T, axis=0, keepdims=True)
        scores = mm(keys, query, NT) * scale + bias
        probs = jnp.exp(scores - lse_ref[head : head + 1, :])
        grad_probs = mm(values, grad, NT)
        dscores = (probs * (grad_probs - delta) * scale).astype(jnp.bfloat16)
        grad_values = mm(probs.astype(jnp.bfloat16), grad, NN)
        grad_keys = mm(dscores, query, NN)
        grad_query = mm(keys, dscores, TN).T.astype(jnp.bfloat16)
        for u in range(2):
            dq_refs[u][:, lanes] = grad_query[u * rows : (u + 1) * rows]
        for k in range(n):
            out = dkv_refs[k]
            out[0, :, lanes] = grad_keys[k * rows : (k + 1) * rows].astype(out.dtype)
            out[1, :, lanes] = grad_values[k * rows : (k + 1) * rows].astype(out.dtype)


def forward_sum_kernel(own_ref, other_ref, out_ref):
    out_ref[...] = (own_ref[...] + other_ref[...].astype(jnp.float32)).astype(jnp.bfloat16)


def unpack_kernel(dq_ref, dq_other_ref, own_ref, part_ref, other_ref, *outs):
    s = lax.axis_index("seq")
    own, other = lane_block(s % 2, dq_ref.shape[1]), lane_block(1 - s % 2, dq_ref.shape[1])
    outs[0][0, :, own] = dq_ref[...]
    outs[0][0, :, other] = dq_other_ref[...]
    for i in range(2):
        total = own_ref[i] + part_ref[i].astype(jnp.float32)
        outs[1 + i][0, :, own] = total.astype(jnp.bfloat16)
        outs[1 + i][0, :, other] = other_ref[i]


def project_kernel(n, w_ref, w2_ref, o_ref, other_ref, *refs):
    (own_ref, *send_refs), (all_ref, parts_ref) = refs[:n], refs[n:]
    s, t = lax.axis_index("seq"), lax.axis_index("tensor")
    rows, heads_width = o_ref.shape[1:]
    own, other = lane_block(s % 2, heads_width), lane_block(1 - s % 2, heads_width)
    for u in range(2):
        all_ref[u * rows : (u + 1) * rows, own] = o_ref[u]
        all_ref[u * rows : (u + 1) * rows, other] = other_ref[1 - u]
    for b, weight_ref in ((0, w_ref), (1, w2_ref)):
        part = mm(all_ref[...], weight_ref[...], NT)
        for u in range(2):
            parts_ref[2 * b + u] = part[u * rows : (u + 1) * rows]
    own_ref[...] = parts_ref[s ^ t]
    for k in range(1, n):
        send_refs[k - 1][...] = parts_ref[s ^ t ^ k].astype(jnp.bfloat16)


def grad_weight_kernel(gate_ref, all_ref, cot_ref, keep_ref, send_ref, outer_ref):
    core, s = lax.axis_index("dp"), lax.axis_index("seq")
    size = all_ref.shape[1]
    half = size // 2
    for b in range(2):
        gate = gate_ref[:, lane_block(s ^ (2 * b), size)]
        cot = jnp.concatenate([cot_ref[2 * b], cot_ref[2 * b + 1]], axis=0)
        grad_proj = (gate * cot.astype(jnp.float32)).astype(jnp.bfloat16)
        outer_ref[...] = mm(grad_proj, all_ref[...], TN)
        keep_ref[b] = outer_ref[pl.ds(pl.multiple_of(core * half, half), half), :]
        send_ref[b] = outer_ref[pl.ds(pl.multiple_of((1 - core) * half, half), half), :].astype(
            jnp.bfloat16
        )


def weight_clips_kernel(keep_ref, other_ref, own_ref, send_ref):
    own_ref[...] = keep_ref[0] + other_ref[0].astype(jnp.float32)
    send_ref[...] = (keep_ref[1] + other_ref[1].astype(jnp.float32)).astype(jnp.bfloat16)


def weight_halves_kernel(own_ref, other_ref, out_ref):
    out_ref[...] = (own_ref[...] + other_ref[...].astype(jnp.float32)).astype(jnp.bfloat16)


def weight_join_kernel(own_ref, other_ref, out_ref):
    core = lax.axis_index("dp")
    half = own_ref.shape[0]
    own = pl.ds(pl.multiple_of(core * half, half), half)
    out_ref[own, :] = own_ref[...].astype(jnp.float32)
    other = pl.ds(pl.multiple_of((1 - core) * half, half), half)
    out_ref[other, :] = other_ref[...].astype(jnp.float32)


def projected_kernel(n, own_ref, *refs):
    parts, out_ref = refs[: n - 1], refs[n - 1]
    projected = own_ref[...]
    for part in parts:
        projected = projected + part[...].astype(jnp.float32)
    out_ref[...] = projected.astype(jnp.bfloat16)


def branch_kernel(gate_ref, cot_ref, projected_ref, branch_ref, gate_grad_ref):
    projected = projected_ref[...].astype(jnp.float32)
    gate = gate_ref[:, lane_block(lax.axis_index("tensor"), projected.shape[1])]
    branch_ref[0] = (gate * projected).astype(jnp.bfloat16)
    cot = cot_ref[0].astype(jnp.float32)
    gate_grad = jnp.sum(cot * projected, axis=0, keepdims=True)
    for i in range(gate_grad_ref.shape[0]):
        gate_grad_ref[i] = gate_grad


def square_shards(
    n, query_rows, key_rows, value_rows, lengths, out_weight, gate_vector, cotangent
):
    tokens, width = query_rows.shape[1:]
    scale = 1.0 / math.sqrt(HD)
    bf16, f32 = jnp.bfloat16, jnp.float32
    shape = jax.ShapeDtypeStruct
    both = ("seq", "tensor")
    both_pairs = [(a, b) for a in range(n) for b in range(n)]

    def permute(value, axes, k):
        return lax.ppermute(value, axes, xor_pairs(n, k))

    def swap(value):
        return lax.ppermute(value, "dp", xor_pairs(2, 1))

    width_half = width // 2
    rows_kv, rows_q = (2, tokens, width_half), (tokens, width_half)
    kv, query, send, near_a, near_b = call(
        pack_kernel,
        [
            shape(rows_kv, bf16),
            shape(rows_q, bf16),
            shape((3, tokens, width_half), bf16),
            *[shape((width_half // 2, width), bf16)] * 2,
        ],
        (query_rows, key_rows, value_rows, out_weight),
        scratch=[pltpu.SemaphoreType.DMA((8,))],
        space=pl.ANY,
        limit=60 * 1024 * 1024,
    )

    def turn(value, k):
        return lax.ppermute(
            value,
            both,
            [
                (a * n + b, ((a & 2) | (b & 1)) * n + (b ^ k ^ ((a ^ b) & 1)))
                for a, b in both_pairs
            ],
        )

    qkv_x, kv_y, near_a, cot_1, cot_2, near_b, cot_late = lax.optimization_barrier(
        (
            permute(send, "seq", 1),
            permute(kv, "seq", 2),
            permute(near_a, "seq", 2),
            turn(cotangent, 1),
            turn(cotangent, 2),
            near_b,
            cotangent,
        )
    )
    kv_xy = permute(qkv_x[:2], "seq", 2)
    kvs = (kv, qkv_x, kv_y, kv_xy)
    block = 2 * tokens
    unit_flops = 2 * n * tokens * block * HD
    wide_flops = 4 * block * width * width
    attended, lse = call(
        functools.partial(forward_kernel, n, scale),
        [shape(rows_kv, bf16), shape((width_half // HD, block), f32)],
        (lengths, *kvs, query),
        flops=6 * unit_flops,
        smem=(0,),
    )
    near_b, cot_0, cot_3, far_a, attended = lax.optimization_barrier(
        (
            permute(near_b, "seq", 2),
            turn(cot_late, 0),
            turn(cot_late, 3),
            swap(near_a),
            attended,
        )
    )
    cots = (cot_0, cot_1, cot_2, cot_3)
    heads = (attended, permute(attended, "seq", 1))
    grad_own, grad_send, cot_all, weight_y = call(
        functools.partial(grad_attended_kernel, n),
        [
            shape(rows_kv, f32),
            shape(rows_kv, bf16),
            shape((n, tokens, width), bf16),
            shape((width, width), bf16),
        ],
        (gate_vector, out_weight, near_a, near_b, far_a, swap(near_b), *cots),
        flops=wide_flops,
        scratch=[pltpu.VMEM((block, width), f32)],
    )
    grad_other = permute(grad_send, "seq", 1)
    *parts, attended_all = call(
        functools.partial(project_kernel, n),
        [
            shape((tokens, width), f32),
            *[shape((tokens, width), bf16)] * (n - 1),
            shape((block, width), bf16),
        ],
        (out_weight, weight_y, *heads),
        flops=wide_flops,
        scratch=[pltpu.VMEM((n, tokens, width), f32)],
    )
    dq, dq_send, dkv, dkv_x, dkv_y, dkv_xy = call(
        functools.partial(backward_kernel, n, scale),
        [shape(rows_q, bf16)] * 2 + [shape(rows_kv, f32)] * 2 + [shape(rows_kv, bf16)] * 2,
        (lengths, lse, attended, grad_own, grad_other, *kvs, query),
        flops=15 * unit_flops,
        smem=(0,),
    )
    keep, send = call(
        grad_weight_kernel,
        [shape((2, width_half, width), f32), shape((2, width_half, width), bf16)],
        (gate_vector, attended_all, cot_all),
        flops=wide_flops,
        scratch=[pltpu.VMEM((width, width), f32)],
    )
    parts = [parts[0]] + [permute(parts[k], "tensor", k) for k in range(1, n)]
    own, send = call(
        weight_clips_kernel,
        [shape((width_half, width), f32), shape((width_half, width), bf16)],
        (keep, swap(send)),
    )
    fin = call(
        weight_halves_kernel, shape((width_half, width), bf16), (own, permute(send, "seq", 2))
    )
    grad_weight = call(weight_join_kernel, shape((width, width), f32), (fin, swap(fin)))
    dq_other, dkv_xy = permute(dq_send, "seq", 1), permute(dkv_xy, "seq", 2)
    dkv_y = permute(dkv_y, "seq", 2)
    dkv_xy, dq_other = lax.optimization_barrier((dkv_xy, dq_other))
    dkv_x = call(forward_sum_kernel, shape(rows_kv, bf16), (dkv_x, dkv_xy))
    dkv_other = permute(dkv_x, "seq", 1)
    projected = call(
        functools.partial(projected_kernel, n), shape((tokens, width), bf16), tuple(parts)
    )
    home = [(a * n + b, (a ^ 1) * n + (b ^ 1) if (a ^ b) & 1 else a * n + b) for a, b in both_pairs]
    projected = lax.ppermute(projected, both, home)
    branch, grad_gate = call(
        branch_kernel,
        [shape((1, tokens, width), bf16), shape((n, 1, width), f32)],
        (gate_vector, cotangent, projected),
    )
    grad_gate = jnp.sum(lax.all_to_all(grad_gate, "seq", 0, 0, tiled=True), axis=0)
    grad_query, grad_key, grad_value = call(
        unpack_kernel,
        [shape((1, tokens, width), bf16)] * 3,
        (dq, dq_other, dkv, dkv_y, dkv_other),
    )
    return (branch, grad_query, grad_key, grad_value, grad_weight, grad_gate)


def solution(mesh):
    placed = (
        P("dp", "seq", "tensor"),
        P("dp", "seq", "tensor"),
        P("dp", "seq", "tensor"),
        P("dp"),
        P("seq", "tensor"),
        P("dp", None),
        P("dp", "seq", "tensor"),
    )
    n = mesh.shape["seq"]

    def body(query_rows, *rest):
        tokens, width = query_rows.shape[1:]
        square = (
            n == 4
            and mesh.shape["tensor"] == n
            and mesh.shape["dp"] == 2
            and width % (2 * HD) == 0
            and tokens % 32 == 0
        )
        if square:
            return square_shards(n, query_rows, *rest)
        return general_shards(query_rows, *rest)

    return jax.shard_map(
        body,
        mesh=mesh,
        in_specs=placed,
        out_specs=(
            P("dp", "seq", "tensor"),
            P("dp", "seq", "tensor"),
            P("dp", "seq", "tensor"),
            P("dp", "seq", "tensor"),
            P("seq", "tensor"),
            P("dp", "tensor"),
        ),
        check_vma=False,
    )
```

```python
import functools
import math

import jax
import jax.numpy as jnp
from jax import lax
from jax.experimental import pallas as pl
from jax.experimental.pallas import tpu as pltpu
from jax.sharding import PartitionSpec as P

HD = 128


MASKED_SCORE = -1e30


def block_rows(piece_rows):
    return math.gcd(piece_rows, 512)


def query_terms(
    query_heads, grad_heads, row_lse, row_delta, key_block, value_block, key_live, score_scale
):
    scores = (
        jnp.einsum("thd,shd->ths", query_heads, key_block, preferred_element_type=jnp.float32)
        * score_scale
    )
    probs = jnp.where(key_live[None, None, :], jnp.exp(scores - row_lse[:, :, None]), 0.0)
    grad_probs = jnp.einsum(
        "thd,shd->ths", grad_heads, value_block, preferred_element_type=jnp.float32
    )
    dscores = (probs * (grad_probs - row_delta[:, :, None]) * score_scale).astype(jnp.bfloat16)
    return jnp.einsum("ths,shd->thd", dscores, key_block, preferred_element_type=jnp.float32)


def key_terms(
    query_block, grad_block, lse_block, delta_block, key_heads, value_heads, key_live, score_scale
):
    scores = (
        jnp.einsum("shd,thd->sht", query_block, key_heads, preferred_element_type=jnp.float32)
        * score_scale
    )
    probs = jnp.where(key_live[None, None, :], jnp.exp(scores - lse_block[:, :, None]), 0.0)
    value_part = jnp.einsum(
        "sht,shd->thd", probs.astype(jnp.bfloat16), grad_block, preferred_element_type=jnp.float32
    )
    grad_probs = jnp.einsum(
        "shd,thd->sht", grad_block, value_heads, preferred_element_type=jnp.float32
    )
    dscores = (probs * (grad_probs - delta_block[:, :, None]) * score_scale).astype(jnp.bfloat16)
    key_part = jnp.einsum("sht,shd->thd", dscores, query_block, preferred_element_type=jnp.float32)
    return (key_part, value_part)


def general_shards(query_rows, key_rows, value_rows, lengths, out_weight, gate_vector, cotangent):
    tokens = query_rows.shape[1]
    local_width = query_rows.shape[2]
    head_count = local_width // HD
    score_scale = 1.0 / math.sqrt(HD)
    length = lengths[0]
    query_local = query_rows[0]
    key_local = key_rows[0]
    value_local = value_rows[0]
    query_heads = query_local.reshape(tokens, head_count, HD)
    key_heads = key_local.reshape(tokens, head_count, HD)
    value_heads = value_local.reshape(tokens, head_count, HD)
    head_zeros = jnp.zeros((tokens, head_count, HD), jnp.float32)
    start_top = jnp.full((tokens, head_count), MASKED_SCORE, jnp.float32)
    start_total = jnp.zeros((tokens, head_count), jnp.float32)
    key_piece = lax.all_gather(key_local, "seq", axis=0, tiled=True)
    value_piece = lax.all_gather(value_local, "seq", axis=0, tiled=True)
    piece_rows = key_piece.shape[0]
    step_rows = block_rows(piece_rows)

    def forward_block_step(block_index, state):
        row_top, row_total, summed = state
        offset = block_index * step_rows
        key_block = lax.dynamic_slice_in_dim(key_piece, offset, step_rows, 0).reshape(
            step_rows, head_count, HD
        )
        value_block = lax.dynamic_slice_in_dim(value_piece, offset, step_rows, 0).reshape(
            step_rows, head_count, HD
        )
        key_live = offset + jnp.arange(step_rows) < length
        scores = (
            jnp.einsum("thd,shd->ths", query_heads, key_block, preferred_element_type=jnp.float32)
            * score_scale
        )
        masked = jnp.where(key_live[None, None, :], scores, MASKED_SCORE)
        new_top = jnp.maximum(row_top, jnp.max(masked, axis=2))
        weights = jnp.where(key_live[None, None, :], jnp.exp(masked - new_top[:, :, None]), 0.0)
        shrink = jnp.exp(row_top - new_top)
        row_total = row_total * shrink + jnp.sum(weights, axis=2)
        summed = summed * shrink[:, :, None] + jnp.einsum(
            "ths,shd->thd",
            weights.astype(jnp.bfloat16),
            value_block,
            preferred_element_type=jnp.float32,
        )
        return (new_top, row_total, summed)

    row_top, row_total, summed = lax.fori_loop(
        0, piece_rows // step_rows, forward_block_step, (start_top, start_total, head_zeros)
    )
    attended_heads = (summed / row_total[:, :, None]).astype(jnp.bfloat16)
    attended = attended_heads.reshape(tokens, local_width)
    row_lse = row_top + jnp.log(row_total)
    weight_whole = lax.all_gather(out_weight, "seq", axis=0, tiled=True)
    partial_value = jnp.einsum(
        "tk,rk->tr", attended, weight_whole, preferred_element_type=jnp.float32
    )
    projected = lax.psum_scatter(
        partial_value.astype(jnp.bfloat16), "tensor", scatter_dimension=1, tiled=True
    ).astype(jnp.float32)
    out_width = projected.shape[1]
    gate_local = lax.dynamic_slice_in_dim(
        gate_vector[0], lax.axis_index("tensor") * out_width, out_width
    )
    cot_rows = cotangent[0].astype(jnp.float32)
    branch = (gate_local[None, :] * projected).astype(jnp.bfloat16)
    gate_grad = lax.psum(jnp.sum(cot_rows * projected, axis=0), "seq")
    grad_proj = (gate_local[None, :] * cot_rows).astype(jnp.bfloat16)
    grad_full = lax.all_gather(grad_proj, "tensor", axis=1, tiled=True)
    grad_att = jnp.dot(grad_full, weight_whole, preferred_element_type=jnp.float32).astype(
        jnp.bfloat16
    )
    row_share = lax.psum_scatter(
        jnp.einsum("tr,tk->rk", grad_full, attended, preferred_element_type=jnp.float32).astype(
            jnp.bfloat16
        ),
        "seq",
        scatter_dimension=0,
        tiled=True,
    )
    grad_weight = lax.psum(row_share, "dp").astype(jnp.float32)
    grad_heads = grad_att.reshape(tokens, head_count, HD)
    row_delta = jnp.sum(grad_heads.astype(jnp.float32) * attended_heads.astype(jnp.float32), axis=2)
    all_lse, all_delta = (
        lax.all_gather(row_lse, "seq", axis=0, tiled=True),
        lax.all_gather(row_delta, "seq", axis=0, tiled=True),
    )
    key_offset = lax.axis_index("seq") * tokens
    local_live = key_offset + jnp.arange(tokens) < length
    query_key_piece = lax.all_gather(key_local, "seq", axis=0, tiled=True)
    query_value_piece = lax.all_gather(value_local, "seq", axis=0, tiled=True)
    piece_rows = query_key_piece.shape[0]
    query_step_rows = block_rows(piece_rows)

    def query_block_step(block_index, state):
        offset = block_index * query_step_rows
        key_block = lax.dynamic_slice_in_dim(query_key_piece, offset, query_step_rows, 0).reshape(
            query_step_rows, head_count, HD
        )
        value_block = lax.dynamic_slice_in_dim(
            query_value_piece, offset, query_step_rows, 0
        ).reshape(query_step_rows, head_count, HD)
        key_live = offset + jnp.arange(query_step_rows) < length
        return state + query_terms(
            query_heads,
            grad_heads,
            row_lse,
            row_delta,
            key_block,
            value_block,
            key_live,
            score_scale,
        )

    grad_q = lax.fori_loop(0, piece_rows // query_step_rows, query_block_step, head_zeros)
    query_piece = lax.all_gather(query_local, "seq", axis=0, tiled=True)
    grad_piece = lax.all_gather(grad_att, "seq", axis=0, tiled=True)
    piece_rows = query_piece.shape[0]
    key_step_rows = block_rows(piece_rows)

    def key_block_step(block_index, state):
        offset = block_index * key_step_rows
        query_block = lax.dynamic_slice_in_dim(query_piece, offset, key_step_rows, 0).reshape(
            key_step_rows, head_count, HD
        )
        grad_block = lax.dynamic_slice_in_dim(grad_piece, offset, key_step_rows, 0).reshape(
            key_step_rows, head_count, HD
        )
        lse_block = lax.dynamic_slice_in_dim(all_lse, offset, key_step_rows, 0)
        delta_block = lax.dynamic_slice_in_dim(all_delta, offset, key_step_rows, 0)
        key_part, value_part = key_terms(
            query_block,
            grad_block,
            lse_block,
            delta_block,
            key_heads,
            value_heads,
            local_live,
            score_scale,
        )
        return (state[0] + key_part, state[1] + value_part)

    grad_k, grad_v = lax.fori_loop(
        0, piece_rows // key_step_rows, key_block_step, (head_zeros, head_zeros)
    )
    grad_query = grad_q.reshape(tokens, local_width).astype(jnp.bfloat16)
    grad_key = grad_k.reshape(tokens, local_width).astype(jnp.bfloat16)
    grad_value = grad_v.reshape(tokens, local_width).astype(jnp.bfloat16)
    return (
        branch[None],
        grad_query[None],
        grad_key[None],
        grad_value[None],
        grad_weight,
        gate_grad[None],
    )


VMEM_LIMIT = 40 * 1024 * 1024
NT = (((1,), (1,)), ((), ()))
TN = (((0,), (0,)), ((), ()))
NN = (((1,), (0,)), ((), ()))


def mm(left, right, dims):
    return lax.dot_general(left, right, dims, preferred_element_type=jnp.float32)


def lane_block(index, width):
    return pl.ds(pl.multiple_of(index * width, HD), width)


def call(kernel, out_shape, args, flops=0, smem=(), scratch=(), space=pltpu.VMEM, out_space=pltpu.VMEM, limit=VMEM_LIMIT):
    nbytes = sum(a.size * a.dtype.itemsize for a in args)
    nbytes += sum(math.prod(o.shape) * o.dtype.itemsize for o in jax.tree.leaves(out_shape))
    return pl.pallas_call(
        kernel,
        out_shape=out_shape,
        in_specs=[
            pl.BlockSpec(memory_space=pltpu.SMEM if i in smem else space)
            for i in range(len(args))
        ],
        out_specs=jax.tree.map(lambda _: pl.BlockSpec(memory_space=out_space), out_shape),
        scratch_shapes=list(scratch),
        compiler_params=pltpu.CompilerParams(vmem_limit_bytes=limit),
        cost_estimate=pl.CostEstimate(flops=flops, bytes_accessed=nbytes, transcendentals=0),
    )(*args)


def xor_pairs(count, k):
    return [(i, i ^ k) for i in range(count)]


def pack_kernel(q_ref, k_ref, v_ref, w_ref, kv_ref, q_own_ref, send_ref, near_ref, near2_ref, sems):
    s, core = lax.axis_index("seq"), lax.axis_index("dp")
    width, quarter = q_own_ref.shape[1], near_ref.shape[0]
    own, other = lane_block(s % 2, width), lane_block(1 - s % 2, width)
    pairs = [
        (k_ref.at[0, :, other], send_ref.at[0]),
        (v_ref.at[0, :, other], send_ref.at[1]),
        (q_ref.at[0, :, other], send_ref.at[2]),
        (k_ref.at[0, :, own], kv_ref.at[0]),
        (v_ref.at[0, :, own], kv_ref.at[1]),
        (q_ref.at[0, :, own], q_own_ref),
    ]
    for i, ref in enumerate((near_ref, near2_ref)):
        at = pl.multiple_of((2 * core + i) * quarter, quarter)
        pairs.append((w_ref.at[pl.ds(at, quarter), :], ref))
    copies = [pltpu.make_async_copy(a, b, sems.at[i]) for i, (a, b) in enumerate(pairs)]
    for copy in copies:
        copy.start()
    for copy in copies:
        copy.wait()


def head_rows(parts, head):
    return jnp.concatenate([p[:, head * HD : (head + 1) * HD] for p in parts], axis=0)


def live_bias(s, n, rows, length):
    parts = []
    for k in range(n):
        place = (s ^ k) * rows + lax.broadcasted_iota(jnp.int32, (rows, 1), 0)
        parts.append(jnp.where(place < length, 0.0, MASKED_SCORE))
    return jnp.concatenate(parts, axis=0)


def forward_kernel(n, scale, len_ref, *refs):
    kvs, queries, (o_ref, lse_ref) = refs[:n], (refs[n], refs[1].at[2]), refs[n + 1 :]
    s = lax.axis_index("seq")
    rows = o_ref.shape[1]
    bias = live_bias(s, n, rows, len_ref[0])
    for head in range(o_ref.shape[2] // HD):
        keys = head_rows([kv.at[0] for kv in kvs], head)
        values = head_rows([kv.at[1] for kv in kvs], head)
        scores = mm(keys, head_rows(queries, head), NT) * scale + bias
        top = jnp.max(scores, axis=0, keepdims=True)
        weights = jnp.exp(scores - top)
        total = jnp.sum(weights, axis=0, keepdims=True)
        summed = mm(values, weights.astype(jnp.bfloat16), TN)
        attended = (summed / total).T.astype(jnp.bfloat16)
        lse_ref[head : head + 1, :] = top + jnp.log(total)
        for u in range(2):
            o_ref[u, :, head * HD : (head + 1) * HD] = attended[u * rows : (u + 1) * rows]


def join_quarters(core, own_refs, other_refs, out_ref):
    rows = own_refs[0].shape[0]
    for i in range(2):
        at = pl.multiple_of((2 * core + i) * rows, rows)
        out_ref[pl.ds(at, rows), :] = own_refs[i][...]
        at = pl.multiple_of((2 * (1 - core) + i) * rows, rows)
        out_ref[pl.ds(at, rows), :] = other_refs[i][...]


def grad_attended_kernel(n, gate_ref, w_ref, *refs):
    quarters, cots, (own_ref, send_ref, cot_ref, w2_ref, share_ref) = refs[:4], refs[4 : 4 + n], refs[4 + n :]
    s = lax.axis_index("seq")
    rows, heads_width = own_ref.shape[1:]
    size = w_ref.shape[0]
    t = lax.axis_index("tensor")
    join_quarters(lax.axis_index("dp"), quarters[:2], quarters[2:], w2_ref)
    for k in range(n):
        cot_ref[s ^ t ^ k] = cots[k][0]
    total = None
    for b, weight_ref in ((0, w_ref), (1, w2_ref)):
        gate = gate_ref[:, lane_block(s ^ (2 * b), size)]
        cot = jnp.concatenate([cot_ref[2 * b], cot_ref[2 * b + 1]], axis=0)
        grad_proj = (gate * cot.astype(jnp.float32)).astype(jnp.bfloat16)
        part = mm(grad_proj, weight_ref[...], NN)
        total = part if total is None else total + part
    share_ref[...] = total
    own, other = lane_block(s % 2, heads_width), lane_block(1 - s % 2, heads_width)
    for u in range(2):
        own_ref[u] = share_ref[u * rows : (u + 1) * rows, own]
        send_ref[1 - u] = share_ref[u * rows : (u + 1) * rows, other].astype(jnp.bfloat16)


def backward_kernel(n, scale, len_ref, lse_ref, o_ref, own_ref, other_ref, *refs):
    kvs, queries = refs[:n], (refs[n], refs[1].at[2])
    dq_refs, dkv_refs = refs[n + 1 : n + 3], refs[n + 3 :]
    s = lax.axis_index("seq")
    rows = o_ref.shape[1]
    bias = live_bias(s, n, rows, len_ref[0])
    for head in range(o_ref.shape[2] // HD):
        lanes = slice(head * HD, (head + 1) * HD)
        keys = head_rows([kv.at[0] for kv in kvs], head)
        values = head_rows([kv.at[1] for kv in kvs], head)
        query = head_rows(queries, head)
        grad = jnp.concatenate(
            [own_ref[u, :, lanes] + other_ref[u, :, lanes].astype(jnp.float32) for u in range(2)],
            axis=0,
        ).astype(jnp.bfloat16)
        attended = jnp.concatenate([o_ref[u, :, lanes] for u in range(2)], axis=0)
        product = grad.astype(jnp.float32) * attended.astype(jnp.float32)
        delta = jnp.sum(product.T, axis=0, keepdims=True)
        scores = mm(keys, query, NT) * scale + bias
        probs = jnp.exp(scores - lse_ref[head : head + 1, :])
        grad_probs = mm(values, grad, NT)
        dscores = (probs * (grad_probs - delta) * scale).astype(jnp.bfloat16)
        grad_values = mm(probs.astype(jnp.bfloat16), grad, NN)
        grad_keys = mm(dscores, query, NN)
        grad_query = mm(keys, dscores, TN).T.astype(jnp.bfloat16)
        for u in range(2):
            dq_refs[u][:, lanes] = grad_query[u * rows : (u + 1) * rows]
        for k in range(n):
            out = dkv_refs[k]
            out[0, :, lanes] = grad_keys[k * rows : (k + 1) * rows].astype(out.dtype)
            out[1, :, lanes] = grad_values[k * rows : (k + 1) * rows].astype(out.dtype)


def forward_sum_kernel(own_ref, other_ref, out_ref):
    out_ref[...] = (own_ref[...] + other_ref[...].astype(jnp.float32)).astype(jnp.bfloat16)


def unpack_kernel(dq_ref, dq_other_ref, own_ref, part_ref, other_ref, *outs):
    s = lax.axis_index("seq")
    own, other = lane_block(s % 2, dq_ref.shape[1]), lane_block(1 - s % 2, dq_ref.shape[1])
    outs[0][0, :, own] = dq_ref[...]
    outs[0][0, :, other] = dq_other_ref[...]
    for i in range(2):
        total = own_ref[i] + part_ref[i].astype(jnp.float32)
        outs[1 + i][0, :, own] = total.astype(jnp.bfloat16)
        outs[1 + i][0, :, other] = other_ref[i]


def project_kernel(n, w_ref, w2_ref, o_ref, other_ref, *refs):
    (own_ref, *send_refs), (all_ref, parts_ref) = refs[:n], refs[n:]
    s, t = lax.axis_index("seq"), lax.axis_index("tensor")
    rows, heads_width = o_ref.shape[1:]
    own, other = lane_block(s % 2, heads_width), lane_block(1 - s % 2, heads_width)
    for u in range(2):
        all_ref[u * rows : (u + 1) * rows, own] = o_ref[u]
        all_ref[u * rows : (u + 1) * rows, other] = other_ref[1 - u]
    for b, weight_ref in ((0, w_ref), (1, w2_ref)):
        part = mm(all_ref[...], weight_ref[...], NT)
        for u in range(2):
            parts_ref[2 * b + u] = part[u * rows : (u + 1) * rows]
    own_ref[...] = parts_ref[s ^ t]
    for k in range(1, n):
        send_refs[k - 1][...] = parts_ref[s ^ t ^ k].astype(jnp.bfloat16)


def grad_weight_kernel(gate_ref, all_ref, cot_ref, keep_ref, send_ref, outer_ref):
    core, s = lax.axis_index("dp"), lax.axis_index("seq")
    size = all_ref.shape[1]
    half = size // 2
    for b in range(2):
        gate = gate_ref[:, lane_block(s ^ (2 * b), size)]
        cot = jnp.concatenate([cot_ref[2 * b], cot_ref[2 * b + 1]], axis=0)
        grad_proj = (gate * cot.astype(jnp.float32)).astype(jnp.bfloat16)
        outer_ref[...] = mm(grad_proj, all_ref[...], TN)
        keep_ref[b] = outer_ref[pl.ds(pl.multiple_of(core * half, half), half), :]
        send_ref[b] = outer_ref[pl.ds(pl.multiple_of((1 - core) * half, half), half), :].astype(
            jnp.bfloat16
        )


def weight_clips_kernel(keep_ref, other_ref, own_ref, send_ref):
    own_ref[...] = keep_ref[0] + other_ref[0].astype(jnp.float32)
    send_ref[...] = (keep_ref[1] + other_ref[1].astype(jnp.float32)).astype(jnp.bfloat16)


def weight_halves_kernel(own_ref, other_ref, out_ref):
    out_ref[...] = (own_ref[...] + other_ref[...].astype(jnp.float32)).astype(jnp.bfloat16)


def weight_join_kernel(own_ref, other_ref, out_ref):
    core = lax.axis_index("dp")
    half = own_ref.shape[0]
    own = pl.ds(pl.multiple_of(core * half, half), half)
    out_ref[own, :] = own_ref[...].astype(jnp.float32)
    other = pl.ds(pl.multiple_of((1 - core) * half, half), half)
    out_ref[other, :] = other_ref[...].astype(jnp.float32)


def projected_kernel(n, own_ref, *refs):
    parts, out_ref = refs[: n - 1], refs[n - 1]
    projected = own_ref[...]
    for part in parts:
        projected = projected + part[...].astype(jnp.float32)
    out_ref[...] = projected.astype(jnp.bfloat16)


def branch_kernel(gate_ref, cot_ref, projected_ref, branch_ref, gate_grad_ref):
    projected = projected_ref[...].astype(jnp.float32)
    gate = gate_ref[:, lane_block(lax.axis_index("tensor"), projected.shape[1])]
    branch_ref[0] = (gate * projected).astype(jnp.bfloat16)
    cot = cot_ref[0].astype(jnp.float32)
    gate_grad = jnp.sum(cot * projected, axis=0, keepdims=True)
    for i in range(gate_grad_ref.shape[0]):
        gate_grad_ref[i] = gate_grad


def square_shards(
    n, query_rows, key_rows, value_rows, lengths, out_weight, gate_vector, cotangent
):
    tokens, width = query_rows.shape[1:]
    scale = 1.0 / math.sqrt(HD)
    bf16, f32 = jnp.bfloat16, jnp.float32
    shape = jax.ShapeDtypeStruct
    both = ("seq", "tensor")
    both_pairs = [(a, b) for a in range(n) for b in range(n)]

    def permute(value, axes, k):
        return lax.ppermute(value, axes, xor_pairs(n, k))

    def swap(value):
        return lax.ppermute(value, "dp", xor_pairs(2, 1))

    width_half = width // 2
    rows_kv, rows_q = (2, tokens, width_half), (tokens, width_half)
    kv, query, send, near_a, near_b = call(
        pack_kernel,
        [
            shape(rows_kv, bf16),
            shape(rows_q, bf16),
            shape((3, tokens, width_half), bf16),
            *[shape((width_half // 2, width), bf16)] * 2,
        ],
        (query_rows, key_rows, value_rows, out_weight),
        scratch=[pltpu.SemaphoreType.DMA((8,))],
        space=pl.ANY,
        limit=60 * 1024 * 1024,
    )

    def turn(value, k):
        return lax.ppermute(
            value,
            both,
            [
                (a * n + b, ((a & 2) | (b & 1)) * n + (b ^ k ^ ((a ^ b) & 1)))
                for a, b in both_pairs
            ],
        )

    qkv_x, kv_y, near_a, cot_1, cot_2, near_b, cot_late = lax.optimization_barrier(
        (
            permute(send, "seq", 1),
            permute(kv, "seq", 2),
            permute(near_a, "seq", 2),
            turn(cotangent, 1),
            turn(cotangent, 2),
            near_b,
            cotangent,
        )
    )
    kv_xy = permute(qkv_x[:2], "seq", 2)
    kvs = (kv, qkv_x, kv_y, kv_xy)
    block = 2 * tokens
    unit_flops = 2 * n * tokens * block * HD
    wide_flops = 4 * block * width * width
    attended, lse = call(
        functools.partial(forward_kernel, n, scale),
        [shape(rows_kv, bf16), shape((width_half // HD, block), f32)],
        (lengths, *kvs, query),
        flops=6 * unit_flops,
        smem=(0,),
    )
    near_b, cot_0, cot_3, far_a, attended = lax.optimization_barrier(
        (
            permute(near_b, "seq", 2),
            turn(cot_late, 0),
            turn(cot_late, 3),
            swap(near_a),
            attended,
        )
    )
    cots = (cot_0, cot_1, cot_2, cot_3)
    heads = (attended, permute(attended, "seq", 1))
    grad_own, grad_send, cot_all, weight_y = call(
        functools.partial(grad_attended_kernel, n),
        [
            shape(rows_kv, f32),
            shape(rows_kv, bf16),
            shape((n, tokens, width), bf16),
            shape((width, width), bf16),
        ],
        (gate_vector, out_weight, near_a, near_b, far_a, swap(near_b), *cots),
        flops=wide_flops,
        scratch=[pltpu.VMEM((block, width), f32)],
    )
    grad_other = permute(grad_send, "seq", 1)
    *parts, attended_all = call(
        functools.partial(project_kernel, n),
        [
            shape((tokens, width), f32),
            *[shape((tokens, width), bf16)] * (n - 1),
            shape((block, width), bf16),
        ],
        (out_weight, weight_y, *heads),
        flops=wide_flops,
        scratch=[pltpu.VMEM((n, tokens, width), f32)],
    )
    dq, dq_send, dkv, dkv_x, dkv_y, dkv_xy = call(
        functools.partial(backward_kernel, n, scale),
        [shape(rows_q, bf16)] * 2 + [shape(rows_kv, f32)] * 2 + [shape(rows_kv, bf16)] * 2,
        (lengths, lse, attended, grad_own, grad_other, *kvs, query),
        flops=15 * unit_flops,
        smem=(0,),
    )
    keep, send = call(
        grad_weight_kernel,
        [shape((2, width_half, width), f32), shape((2, width_half, width), bf16)],
        (gate_vector, attended_all, cot_all),
        flops=wide_flops,
        scratch=[pltpu.VMEM((width, width), f32)],
    )
    parts = [parts[0]] + [permute(parts[k], "tensor", k) for k in range(1, n)]
    own, send = call(
        weight_clips_kernel,
        [shape((width_half, width), f32), shape((width_half, width), bf16)],
        (keep, swap(send)),
    )
    fin = call(
        weight_halves_kernel, shape((width_half, width), bf16), (own, permute(send, "seq", 2))
    )
    grad_weight = call(weight_join_kernel, shape((width, width), f32), (fin, swap(fin)))
    dq_other, dkv_xy = permute(dq_send, "seq", 1), permute(dkv_xy, "seq", 2)
    dkv_y = permute(dkv_y, "seq", 2)
    dkv_xy, dq_other = lax.optimization_barrier((dkv_xy, dq_other))
    dkv_x = call(forward_sum_kernel, shape(rows_kv, bf16), (dkv_x, dkv_xy))
    dkv_other = permute(dkv_x, "seq", 1)
    projected = call(
        functools.partial(projected_kernel, n), shape((tokens, width), bf16), tuple(parts)
    )
    home = [(a * n + b, (a ^ 1) * n + (b ^ 1) if (a ^ b) & 1 else a * n + b) for a, b in both_pairs]
    projected = lax.ppermute(projected, both, home)
    projected, grad_weight = lax.optimization_barrier((projected, grad_weight))
    branch, grad_gate = call(
        branch_kernel,
        [shape((1, tokens, width), bf16), shape((n, 1, width), f32)],
        (gate_vector, cotangent, projected),
    )
    grad_gate = jnp.sum(lax.all_to_all(grad_gate, "seq", 0, 0, tiled=True), axis=0)
    grad_query, grad_key, grad_value = call(
        unpack_kernel,
        [shape((1, tokens, width), bf16)] * 3,
        (dq, dq_other, dkv, dkv_y, dkv_other),
    )
    return (branch, grad_query, grad_key, grad_value, grad_weight, grad_gate)


def solution(mesh):
    placed = (
        P("dp", "seq", "tensor"),
        P("dp", "seq", "tensor"),
        P("dp", "seq", "tensor"),
        P("dp"),
        P("seq", "tensor"),
        P("dp", None),
        P("dp", "seq", "tensor"),
    )
    n = mesh.shape["seq"]

    def body(query_rows, *rest):
        tokens, width = query_rows.shape[1:]
        square = (
            n == 4
            and mesh.shape["tensor"] == n
            and mesh.shape["dp"] == 2
            and width % (2 * HD) == 0
            and tokens % 32 == 0
        )
        if square:
            return square_shards(n, query_rows, *rest)
        return general_shards(query_rows, *rest)

    return jax.shard_map(
        body,
        mesh=mesh,
        in_specs=placed,
        out_specs=(
            P("dp", "seq", "tensor"),
            P("dp", "seq", "tensor"),
            P("dp", "seq", "tensor"),
            P("dp", "seq", "tensor"),
            P("seq", "tensor"),
            P("dp", "tensor"),
        ),
        check_vma=False,
    )
```

```python
import functools
import math

import jax
import jax.numpy as jnp
from jax import lax
from jax.experimental import pallas as pl
from jax.experimental.pallas import tpu as pltpu
from jax.sharding import PartitionSpec as P

HD = 128


MASKED_SCORE = -1e30


def block_rows(piece_rows):
    return math.gcd(piece_rows, 512)


def query_terms(
    query_heads, grad_heads, row_lse, row_delta, key_block, value_block, key_live, score_scale
):
    scores = (
        jnp.einsum("thd,shd->ths", query_heads, key_block, preferred_element_type=jnp.float32)
        * score_scale
    )
    probs = jnp.where(key_live[None, None, :], jnp.exp(scores - row_lse[:, :, None]), 0.0)
    grad_probs = jnp.einsum(
        "thd,shd->ths", grad_heads, value_block, preferred_element_type=jnp.float32
    )
    dscores = (probs * (grad_probs - row_delta[:, :, None]) * score_scale).astype(jnp.bfloat16)
    return jnp.einsum("ths,shd->thd", dscores, key_block, preferred_element_type=jnp.float32)


def key_terms(
    query_block, grad_block, lse_block, delta_block, key_heads, value_heads, key_live, score_scale
):
    scores = (
        jnp.einsum("shd,thd->sht", query_block, key_heads, preferred_element_type=jnp.float32)
        * score_scale
    )
    probs = jnp.where(key_live[None, None, :], jnp.exp(scores - lse_block[:, :, None]), 0.0)
    value_part = jnp.einsum(
        "sht,shd->thd", probs.astype(jnp.bfloat16), grad_block, preferred_element_type=jnp.float32
    )
    grad_probs = jnp.einsum(
        "shd,thd->sht", grad_block, value_heads, preferred_element_type=jnp.float32
    )
    dscores = (probs * (grad_probs - delta_block[:, :, None]) * score_scale).astype(jnp.bfloat16)
    key_part = jnp.einsum("sht,shd->thd", dscores, query_block, preferred_element_type=jnp.float32)
    return (key_part, value_part)


def general_shards(query_rows, key_rows, value_rows, lengths, out_weight, gate_vector, cotangent):
    tokens = query_rows.shape[1]
    local_width = query_rows.shape[2]
    head_count = local_width // HD
    score_scale = 1.0 / math.sqrt(HD)
    length = lengths[0]
    query_local = query_rows[0]
    key_local = key_rows[0]
    value_local = value_rows[0]
    query_heads = query_local.reshape(tokens, head_count, HD)
    key_heads = key_local.reshape(tokens, head_count, HD)
    value_heads = value_local.reshape(tokens, head_count, HD)
    head_zeros = jnp.zeros((tokens, head_count, HD), jnp.float32)
    start_top = jnp.full((tokens, head_count), MASKED_SCORE, jnp.float32)
    start_total = jnp.zeros((tokens, head_count), jnp.float32)
    key_piece = lax.all_gather(key_local, "seq", axis=0, tiled=True)
    value_piece = lax.all_gather(value_local, "seq", axis=0, tiled=True)
    piece_rows = key_piece.shape[0]
    step_rows = block_rows(piece_rows)

    def forward_block_step(block_index, state):
        row_top, row_total, summed = state
        offset = block_index * step_rows
        key_block = lax.dynamic_slice_in_dim(key_piece, offset, step_rows, 0).reshape(
            step_rows, head_count, HD
        )
        value_block = lax.dynamic_slice_in_dim(value_piece, offset, step_rows, 0).reshape(
            step_rows, head_count, HD
        )
        key_live = offset + jnp.arange(step_rows) < length
        scores = (
            jnp.einsum("thd,shd->ths", query_heads, key_block, preferred_element_type=jnp.float32)
            * score_scale
        )
        masked = jnp.where(key_live[None, None, :], scores, MASKED_SCORE)
        new_top = jnp.maximum(row_top, jnp.max(masked, axis=2))
        weights = jnp.where(key_live[None, None, :], jnp.exp(masked - new_top[:, :, None]), 0.0)
        shrink = jnp.exp(row_top - new_top)
        row_total = row_total * shrink + jnp.sum(weights, axis=2)
        summed = summed * shrink[:, :, None] + jnp.einsum(
            "ths,shd->thd",
            weights.astype(jnp.bfloat16),
            value_block,
            preferred_element_type=jnp.float32,
        )
        return (new_top, row_total, summed)

    row_top, row_total, summed = lax.fori_loop(
        0, piece_rows // step_rows, forward_block_step, (start_top, start_total, head_zeros)
    )
    attended_heads = (summed / row_total[:, :, None]).astype(jnp.bfloat16)
    attended = attended_heads.reshape(tokens, local_width)
    row_lse = row_top + jnp.log(row_total)
    weight_whole = lax.all_gather(out_weight, "seq", axis=0, tiled=True)
    partial_value = jnp.einsum(
        "tk,rk->tr", attended, weight_whole, preferred_element_type=jnp.float32
    )
    projected = lax.psum_scatter(
        partial_value.astype(jnp.bfloat16), "tensor", scatter_dimension=1, tiled=True
    ).astype(jnp.float32)
    out_width = projected.shape[1]
    gate_local = lax.dynamic_slice_in_dim(
        gate_vector[0], lax.axis_index("tensor") * out_width, out_width
    )
    cot_rows = cotangent[0].astype(jnp.float32)
    branch = (gate_local[None, :] * projected).astype(jnp.bfloat16)
    gate_grad = lax.psum(jnp.sum(cot_rows * projected, axis=0), "seq")
    grad_proj = (gate_local[None, :] * cot_rows).astype(jnp.bfloat16)
    grad_full = lax.all_gather(grad_proj, "tensor", axis=1, tiled=True)
    grad_att = jnp.dot(grad_full, weight_whole, preferred_element_type=jnp.float32).astype(
        jnp.bfloat16
    )
    row_share = lax.psum_scatter(
        jnp.einsum("tr,tk->rk", grad_full, attended, preferred_element_type=jnp.float32).astype(
            jnp.bfloat16
        ),
        "seq",
        scatter_dimension=0,
        tiled=True,
    )
    grad_weight = lax.psum(row_share, "dp").astype(jnp.float32)
    grad_heads = grad_att.reshape(tokens, head_count, HD)
    row_delta = jnp.sum(grad_heads.astype(jnp.float32) * attended_heads.astype(jnp.float32), axis=2)
    all_lse, all_delta = (
        lax.all_gather(row_lse, "seq", axis=0, tiled=True),
        lax.all_gather(row_delta, "seq", axis=0, tiled=True),
    )
    key_offset = lax.axis_index("seq") * tokens
    local_live = key_offset + jnp.arange(tokens) < length
    query_key_piece = lax.all_gather(key_local, "seq", axis=0, tiled=True)
    query_value_piece = lax.all_gather(value_local, "seq", axis=0, tiled=True)
    piece_rows = query_key_piece.shape[0]
    query_step_rows = block_rows(piece_rows)

    def query_block_step(block_index, state):
        offset = block_index * query_step_rows
        key_block = lax.dynamic_slice_in_dim(query_key_piece, offset, query_step_rows, 0).reshape(
            query_step_rows, head_count, HD
        )
        value_block = lax.dynamic_slice_in_dim(
            query_value_piece, offset, query_step_rows, 0
        ).reshape(query_step_rows, head_count, HD)
        key_live = offset + jnp.arange(query_step_rows) < length
        return state + query_terms(
            query_heads,
            grad_heads,
            row_lse,
            row_delta,
            key_block,
            value_block,
            key_live,
            score_scale,
        )

    grad_q = lax.fori_loop(0, piece_rows // query_step_rows, query_block_step, head_zeros)
    query_piece = lax.all_gather(query_local, "seq", axis=0, tiled=True)
    grad_piece = lax.all_gather(grad_att, "seq", axis=0, tiled=True)
    piece_rows = query_piece.shape[0]
    key_step_rows = block_rows(piece_rows)

    def key_block_step(block_index, state):
        offset = block_index * key_step_rows
        query_block = lax.dynamic_slice_in_dim(query_piece, offset, key_step_rows, 0).reshape(
            key_step_rows, head_count, HD
        )
        grad_block = lax.dynamic_slice_in_dim(grad_piece, offset, key_step_rows, 0).reshape(
            key_step_rows, head_count, HD
        )
        lse_block = lax.dynamic_slice_in_dim(all_lse, offset, key_step_rows, 0)
        delta_block = lax.dynamic_slice_in_dim(all_delta, offset, key_step_rows, 0)
        key_part, value_part = key_terms(
            query_block,
            grad_block,
            lse_block,
            delta_block,
            key_heads,
            value_heads,
            local_live,
            score_scale,
        )
        return (state[0] + key_part, state[1] + value_part)

    grad_k, grad_v = lax.fori_loop(
        0, piece_rows // key_step_rows, key_block_step, (head_zeros, head_zeros)
    )
    grad_query = grad_q.reshape(tokens, local_width).astype(jnp.bfloat16)
    grad_key = grad_k.reshape(tokens, local_width).astype(jnp.bfloat16)
    grad_value = grad_v.reshape(tokens, local_width).astype(jnp.bfloat16)
    return (
        branch[None],
        grad_query[None],
        grad_key[None],
        grad_value[None],
        grad_weight,
        gate_grad[None],
    )


VMEM_LIMIT = 40 * 1024 * 1024
NT = (((1,), (1,)), ((), ()))
TN = (((0,), (0,)), ((), ()))
NN = (((1,), (0,)), ((), ()))


def mm(left, right, dims):
    return lax.dot_general(left, right, dims, preferred_element_type=jnp.float32)


def lane_block(index, width):
    return pl.ds(pl.multiple_of(index * width, HD), width)


def call(kernel, out_shape, args, flops=0, smem=(), scratch=(), space=pltpu.VMEM, out_space=pltpu.VMEM, limit=VMEM_LIMIT):
    nbytes = sum(a.size * a.dtype.itemsize for a in args)
    nbytes += sum(math.prod(o.shape) * o.dtype.itemsize for o in jax.tree.leaves(out_shape))
    return pl.pallas_call(
        kernel,
        out_shape=out_shape,
        in_specs=[
            pl.BlockSpec(memory_space=pltpu.SMEM if i in smem else space)
            for i in range(len(args))
        ],
        out_specs=jax.tree.map(lambda _: pl.BlockSpec(memory_space=out_space), out_shape),
        scratch_shapes=list(scratch),
        compiler_params=pltpu.CompilerParams(vmem_limit_bytes=limit),
        cost_estimate=pl.CostEstimate(flops=flops, bytes_accessed=nbytes, transcendentals=0),
    )(*args)


def xor_pairs(count, k):
    return [(i, i ^ k) for i in range(count)]


def pack_kernel(q_ref, k_ref, v_ref, w_ref, kv_ref, q_own_ref, send_ref, near_ref, near2_ref, sems):
    s, core = lax.axis_index("seq"), lax.axis_index("dp")
    width, quarter = q_own_ref.shape[1], near_ref.shape[0]
    own, other = lane_block(s % 2, width), lane_block(1 - s % 2, width)
    pairs = [
        (k_ref.at[0, :, other], send_ref.at[0]),
        (v_ref.at[0, :, other], send_ref.at[1]),
        (q_ref.at[0, :, other], send_ref.at[2]),
        (k_ref.at[0, :, own], kv_ref.at[0]),
        (v_ref.at[0, :, own], kv_ref.at[1]),
        (q_ref.at[0, :, own], q_own_ref),
    ]
    for i, ref in enumerate((near_ref, near2_ref)):
        at = pl.multiple_of((2 * core + i) * quarter, quarter)
        pairs.append((w_ref.at[pl.ds(at, quarter), :], ref))
    copies = [pltpu.make_async_copy(a, b, sems.at[i]) for i, (a, b) in enumerate(pairs)]
    for copy in copies:
        copy.start()
    for copy in copies:
        copy.wait()


def head_rows(parts, head):
    return jnp.concatenate([p[:, head * HD : (head + 1) * HD] for p in parts], axis=0)


def live_bias(s, n, rows, length):
    parts = []
    for k in range(n):
        place = (s ^ k) * rows + lax.broadcasted_iota(jnp.int32, (rows, 1), 0)
        parts.append(jnp.where(place < length, 0.0, MASKED_SCORE))
    return jnp.concatenate(parts, axis=0)


def forward_kernel(n, scale, len_ref, *refs):
    kvs, queries, (o_ref, lse_ref) = refs[:n], (refs[n], refs[1].at[2]), refs[n + 1 :]
    s = lax.axis_index("seq")
    rows = o_ref.shape[1]
    bias = live_bias(s, n, rows, len_ref[0])
    for head in range(o_ref.shape[2] // HD):
        keys = head_rows([kv.at[0] for kv in kvs], head)
        values = head_rows([kv.at[1] for kv in kvs], head)
        scores = mm(keys, head_rows(queries, head), NT) * scale + bias
        top = jnp.max(scores, axis=0, keepdims=True)
        weights = jnp.exp(scores - top)
        total = jnp.sum(weights, axis=0, keepdims=True)
        summed = mm(values, weights.astype(jnp.bfloat16), TN)
        attended = (summed / total).T.astype(jnp.bfloat16)
        lse_ref[head : head + 1, :] = top + jnp.log(total)
        for u in range(2):
            o_ref[u, :, head * HD : (head + 1) * HD] = attended[u * rows : (u + 1) * rows]


def join_quarters(core, own_refs, other_refs, out_ref):
    rows = own_refs[0].shape[0]
    for i in range(2):
        at = pl.multiple_of((2 * core + i) * rows, rows)
        out_ref[pl.ds(at, rows), :] = own_refs[i][...]
        at = pl.multiple_of((2 * (1 - core) + i) * rows, rows)
        out_ref[pl.ds(at, rows), :] = other_refs[i][...]


def grad_attended_kernel(n, gate_ref, w_ref, *refs):
    quarters, cots, (own_ref, send_ref, cot_ref, w2_ref, share_ref) = refs[:4], refs[4 : 4 + n], refs[4 + n :]
    s = lax.axis_index("seq")
    rows, heads_width = own_ref.shape[1:]
    size = w_ref.shape[0]
    t = lax.axis_index("tensor")
    join_quarters(lax.axis_index("dp"), quarters[:2], quarters[2:], w2_ref)
    for k in range(n):
        cot_ref[s ^ t ^ k] = cots[k][0]
    total = None
    for b, weight_ref in ((0, w_ref), (1, w2_ref)):
        gate = gate_ref[:, lane_block(s ^ (2 * b), size)]
        cot = jnp.concatenate([cot_ref[2 * b], cot_ref[2 * b + 1]], axis=0)
        grad_proj = (gate * cot.astype(jnp.float32)).astype(jnp.bfloat16)
        part = mm(grad_proj, weight_ref[...], NN)
        total = part if total is None else total + part
    share_ref[...] = total
    own, other = lane_block(s % 2, heads_width), lane_block(1 - s % 2, heads_width)
    for u in range(2):
        own_ref[u] = share_ref[u * rows : (u + 1) * rows, own]
        send_ref[1 - u] = share_ref[u * rows : (u + 1) * rows, other].astype(jnp.bfloat16)


def backward_kernel(n, scale, len_ref, lse_ref, o_ref, own_ref, other_ref, *refs):
    kvs, queries = refs[:n], (refs[n], refs[1].at[2])
    dq_refs, dkv_refs = refs[n + 1 : n + 3], refs[n + 3 :]
    s = lax.axis_index("seq")
    rows = o_ref.shape[1]
    bias = live_bias(s, n, rows, len_ref[0])
    for head in range(o_ref.shape[2] // HD):
        lanes = slice(head * HD, (head + 1) * HD)
        keys = head_rows([kv.at[0] for kv in kvs], head)
        values = head_rows([kv.at[1] for kv in kvs], head)
        query = head_rows(queries, head)
        grad = jnp.concatenate(
            [own_ref[u, :, lanes] + other_ref[u, :, lanes].astype(jnp.float32) for u in range(2)],
            axis=0,
        ).astype(jnp.bfloat16)
        attended = jnp.concatenate([o_ref[u, :, lanes] for u in range(2)], axis=0)
        product = grad.astype(jnp.float32) * attended.astype(jnp.float32)
        delta = jnp.sum(product.T, axis=0, keepdims=True)
        scores = mm(keys, query, NT) * scale + bias
        probs = jnp.exp(scores - lse_ref[head : head + 1, :])
        grad_probs = mm(values, grad, NT)
        dscores = (probs * (grad_probs - delta) * scale).astype(jnp.bfloat16)
        grad_values = mm(probs.astype(jnp.bfloat16), grad, NN)
        grad_keys = mm(dscores, query, NN)
        grad_query = mm(keys, dscores, TN).T.astype(jnp.bfloat16)
        for u in range(2):
            dq_refs[u][:, lanes] = grad_query[u * rows : (u + 1) * rows]
        for k in range(n):
            out = dkv_refs[k]
            out[0, :, lanes] = grad_keys[k * rows : (k + 1) * rows].astype(out.dtype)
            out[1, :, lanes] = grad_values[k * rows : (k + 1) * rows].astype(out.dtype)


def forward_sum_kernel(own_ref, other_ref, out_ref):
    out_ref[...] = (own_ref[...] + other_ref[...].astype(jnp.float32)).astype(jnp.bfloat16)


def unpack_kernel(dq_ref, dq_other_ref, own_ref, part_ref, other_ref, *outs):
    s = lax.axis_index("seq")
    own, other = lane_block(s % 2, dq_ref.shape[1]), lane_block(1 - s % 2, dq_ref.shape[1])
    outs[0][0, :, own] = dq_ref[...]
    outs[0][0, :, other] = dq_other_ref[...]
    for i in range(2):
        total = own_ref[i] + part_ref[i].astype(jnp.float32)
        outs[1 + i][0, :, own] = total.astype(jnp.bfloat16)
        outs[1 + i][0, :, other] = other_ref[i]


def project_kernel(n, w_ref, w2_ref, o_ref, other_ref, *refs):
    (own_ref, *send_refs), (all_ref, parts_ref) = refs[:n], refs[n:]
    s, t = lax.axis_index("seq"), lax.axis_index("tensor")
    rows, heads_width = o_ref.shape[1:]
    own, other = lane_block(s % 2, heads_width), lane_block(1 - s % 2, heads_width)
    for u in range(2):
        all_ref[u * rows : (u + 1) * rows, own] = o_ref[u]
        all_ref[u * rows : (u + 1) * rows, other] = other_ref[1 - u]
    for b, weight_ref in ((0, w_ref), (1, w2_ref)):
        part = mm(all_ref[...], weight_ref[...], NT)
        for u in range(2):
            parts_ref[2 * b + u] = part[u * rows : (u + 1) * rows]
    own_ref[...] = parts_ref[s ^ t]
    for k in range(1, n):
        send_refs[k - 1][...] = parts_ref[s ^ t ^ k].astype(jnp.bfloat16)


def grad_weight_kernel(gate_ref, all_ref, cot_ref, keep_ref, send_ref, outer_ref):
    core, s = lax.axis_index("dp"), lax.axis_index("seq")
    size = all_ref.shape[1]
    half = size // 2
    for b in range(2):
        gate = gate_ref[:, lane_block(s ^ (2 * b), size)]
        cot = jnp.concatenate([cot_ref[2 * b], cot_ref[2 * b + 1]], axis=0)
        grad_proj = (gate * cot.astype(jnp.float32)).astype(jnp.bfloat16)
        outer_ref[...] = mm(grad_proj, all_ref[...], TN)
        keep_ref[b] = outer_ref[pl.ds(pl.multiple_of(core * half, half), half), :]
        send_ref[b] = outer_ref[pl.ds(pl.multiple_of((1 - core) * half, half), half), :].astype(
            jnp.bfloat16
        )


def weight_clips_kernel(keep_ref, other_ref, own_ref, send_ref):
    own_ref[...] = keep_ref[0] + other_ref[0].astype(jnp.float32)
    send_ref[...] = (keep_ref[1] + other_ref[1].astype(jnp.float32)).astype(jnp.bfloat16)


def weight_halves_kernel(own_ref, other_ref, out_ref):
    out_ref[...] = (own_ref[...] + other_ref[...].astype(jnp.float32)).astype(jnp.bfloat16)


def weight_join_kernel(own_ref, other_ref, out_ref):
    core = lax.axis_index("dp")
    half = own_ref.shape[0]
    own = pl.ds(pl.multiple_of(core * half, half), half)
    out_ref[own, :] = own_ref[...].astype(jnp.float32)
    other = pl.ds(pl.multiple_of((1 - core) * half, half), half)
    out_ref[other, :] = other_ref[...].astype(jnp.float32)


def projected_kernel(n, own_ref, *refs):
    parts, out_ref = refs[: n - 1], refs[n - 1]
    projected = own_ref[...]
    for part in parts:
        projected = projected + part[...].astype(jnp.float32)
    out_ref[...] = projected.astype(jnp.bfloat16)


def branch_kernel(gate_ref, cot_ref, projected_ref, branch_ref, gate_grad_ref):
    projected = projected_ref[...].astype(jnp.float32)
    gate = gate_ref[:, lane_block(lax.axis_index("tensor"), projected.shape[1])]
    branch_ref[0] = (gate * projected).astype(jnp.bfloat16)
    cot = cot_ref[0].astype(jnp.float32)
    gate_grad = jnp.sum(cot * projected, axis=0, keepdims=True)
    for i in range(gate_grad_ref.shape[0]):
        gate_grad_ref[i] = gate_grad


def square_shards(
    n, query_rows, key_rows, value_rows, lengths, out_weight, gate_vector, cotangent
):
    tokens, width = query_rows.shape[1:]
    scale = 1.0 / math.sqrt(HD)
    bf16, f32 = jnp.bfloat16, jnp.float32
    shape = jax.ShapeDtypeStruct
    both = ("seq", "tensor")
    both_pairs = [(a, b) for a in range(n) for b in range(n)]

    def permute(value, axes, k):
        return lax.ppermute(value, axes, xor_pairs(n, k))

    def swap(value):
        return lax.ppermute(value, "dp", xor_pairs(2, 1))

    width_half = width // 2
    rows_kv, rows_q = (2, tokens, width_half), (tokens, width_half)
    kv, query, send, near_a, near_b = call(
        pack_kernel,
        [
            shape(rows_kv, bf16),
            shape(rows_q, bf16),
            shape((3, tokens, width_half), bf16),
            *[shape((width_half // 2, width), bf16)] * 2,
        ],
        (query_rows, key_rows, value_rows, out_weight),
        scratch=[pltpu.SemaphoreType.DMA((8,))],
        space=pl.ANY,
        limit=60 * 1024 * 1024,
    )

    def turn(value, k):
        return lax.ppermute(
            value,
            both,
            [
                (a * n + b, ((a & 2) | (b & 1)) * n + (b ^ k ^ ((a ^ b) & 1)))
                for a, b in both_pairs
            ],
        )

    qkv_x, kv_y, near_a, cot_1, cot_2, near_b, cot_late = lax.optimization_barrier(
        (
            permute(send, "seq", 1),
            permute(kv, "seq", 2),
            permute(near_a, "seq", 2),
            turn(cotangent, 1),
            turn(cotangent, 2),
            near_b,
            cotangent,
        )
    )
    kv_xy = permute(qkv_x[:2], "seq", 2)
    kvs = (kv, qkv_x, kv_y, kv_xy)
    block = 2 * tokens
    unit_flops = 2 * n * tokens * block * HD
    wide_flops = 4 * block * width * width
    attended, lse = call(
        functools.partial(forward_kernel, n, scale),
        [shape(rows_kv, bf16), shape((width_half // HD, block), f32)],
        (lengths, *kvs, query),
        flops=6 * unit_flops,
        smem=(0,),
    )
    near_b, far_a, attended = lax.optimization_barrier(
        (permute(near_b, "seq", 2), swap(near_a), attended)
    )
    cots = (turn(cot_late, 0), cot_1, cot_2, turn(cot_late, 3))
    heads = (attended, permute(attended, "seq", 1))
    grad_own, grad_send, cot_all, weight_y = call(
        functools.partial(grad_attended_kernel, n),
        [
            shape(rows_kv, f32),
            shape(rows_kv, bf16),
            shape((n, tokens, width), bf16),
            shape((width, width), bf16),
        ],
        (gate_vector, out_weight, near_a, near_b, far_a, swap(near_b), *cots),
        flops=wide_flops,
        scratch=[pltpu.VMEM((block, width), f32)],
    )
    grad_other = permute(grad_send, "seq", 1)
    *parts, attended_all = call(
        functools.partial(project_kernel, n),
        [
            shape((tokens, width), f32),
            *[shape((tokens, width), bf16)] * (n - 1),
            shape((block, width), bf16),
        ],
        (out_weight, weight_y, *heads),
        flops=wide_flops,
        scratch=[pltpu.VMEM((n, tokens, width), f32)],
    )
    dq, dq_send, dkv, dkv_x, dkv_y, dkv_xy = call(
        functools.partial(backward_kernel, n, scale),
        [shape(rows_q, bf16)] * 2 + [shape(rows_kv, f32)] * 2 + [shape(rows_kv, bf16)] * 2,
        (lengths, lse, attended, grad_own, grad_other, *kvs, query),
        flops=15 * unit_flops,
        smem=(0,),
    )
    keep, send = call(
        grad_weight_kernel,
        [shape((2, width_half, width), f32), shape((2, width_half, width), bf16)],
        (gate_vector, attended_all, cot_all),
        flops=wide_flops,
        scratch=[pltpu.VMEM((width, width), f32)],
    )
    parts = [parts[0]] + [permute(parts[k], "tensor", k) for k in range(1, n)]
    own, send = call(
        weight_clips_kernel,
        [shape((width_half, width), f32), shape((width_half, width), bf16)],
        (keep, swap(send)),
    )
    fin = call(
        weight_halves_kernel, shape((width_half, width), bf16), (own, permute(send, "seq", 2))
    )
    grad_weight = call(weight_join_kernel, shape((width, width), f32), (fin, swap(fin)))
    dq_other, dkv_xy = permute(dq_send, "seq", 1), permute(dkv_xy, "seq", 2)
    dkv_y = permute(dkv_y, "seq", 2)
    dkv_xy, dq_other = lax.optimization_barrier((dkv_xy, dq_other))
    dkv_x = call(forward_sum_kernel, shape(rows_kv, bf16), (dkv_x, dkv_xy))
    dkv_other = permute(dkv_x, "seq", 1)
    projected = call(
        functools.partial(projected_kernel, n), shape((tokens, width), bf16), tuple(parts)
    )
    home = [(a * n + b, (a ^ 1) * n + (b ^ 1) if (a ^ b) & 1 else a * n + b) for a, b in both_pairs]
    projected = lax.ppermute(projected, both, home)
    projected, grad_weight = lax.optimization_barrier((projected, grad_weight))
    branch, grad_gate = call(
        branch_kernel,
        [shape((1, tokens, width), bf16), shape((n, 1, width), f32)],
        (gate_vector, cotangent, projected),
    )
    grad_gate = jnp.sum(lax.all_to_all(grad_gate, "seq", 0, 0, tiled=True), axis=0)
    grad_query, grad_key, grad_value = call(
        unpack_kernel,
        [shape((1, tokens, width), bf16)] * 3,
        (dq, dq_other, dkv, dkv_y, dkv_other),
    )
    return (branch, grad_query, grad_key, grad_value, grad_weight, grad_gate)


def solution(mesh):
    placed = (
        P("dp", "seq", "tensor"),
        P("dp", "seq", "tensor"),
        P("dp", "seq", "tensor"),
        P("dp"),
        P("seq", "tensor"),
        P("dp", None),
        P("dp", "seq", "tensor"),
    )
    n = mesh.shape["seq"]

    def body(query_rows, *rest):
        tokens, width = query_rows.shape[1:]
        square = (
            n == 4
            and mesh.shape["tensor"] == n
            and mesh.shape["dp"] == 2
            and width % (2 * HD) == 0
            and tokens % 32 == 0
        )
        if square:
            return square_shards(n, query_rows, *rest)
        return general_shards(query_rows, *rest)

    return jax.shard_map(
        body,
        mesh=mesh,
        in_specs=placed,
        out_specs=(
            P("dp", "seq", "tensor"),
            P("dp", "seq", "tensor"),
            P("dp", "seq", "tensor"),
            P("dp", "seq", "tensor"),
            P("seq", "tensor"),
            P("dp", "tensor"),
        ),
        check_vma=False,
    )
```

```python
import functools
import math

import jax
import jax.numpy as jnp
from jax import lax
from jax.experimental import pallas as pl
from jax.experimental.pallas import tpu as pltpu
from jax.sharding import PartitionSpec as P

HD = 128


MASKED_SCORE = -1e30


def block_rows(piece_rows):
    return math.gcd(piece_rows, 512)


def query_terms(
    query_heads, grad_heads, row_lse, row_delta, key_block, value_block, key_live, score_scale
):
    scores = (
        jnp.einsum("thd,shd->ths", query_heads, key_block, preferred_element_type=jnp.float32)
        * score_scale
    )
    probs = jnp.where(key_live[None, None, :], jnp.exp(scores - row_lse[:, :, None]), 0.0)
    grad_probs = jnp.einsum(
        "thd,shd->ths", grad_heads, value_block, preferred_element_type=jnp.float32
    )
    dscores = (probs * (grad_probs - row_delta[:, :, None]) * score_scale).astype(jnp.bfloat16)
    return jnp.einsum("ths,shd->thd", dscores, key_block, preferred_element_type=jnp.float32)


def key_terms(
    query_block, grad_block, lse_block, delta_block, key_heads, value_heads, key_live, score_scale
):
    scores = (
        jnp.einsum("shd,thd->sht", query_block, key_heads, preferred_element_type=jnp.float32)
        * score_scale
    )
    probs = jnp.where(key_live[None, None, :], jnp.exp(scores - lse_block[:, :, None]), 0.0)
    value_part = jnp.einsum(
        "sht,shd->thd", probs.astype(jnp.bfloat16), grad_block, preferred_element_type=jnp.float32
    )
    grad_probs = jnp.einsum(
        "shd,thd->sht", grad_block, value_heads, preferred_element_type=jnp.float32
    )
    dscores = (probs * (grad_probs - delta_block[:, :, None]) * score_scale).astype(jnp.bfloat16)
    key_part = jnp.einsum("sht,shd->thd", dscores, query_block, preferred_element_type=jnp.float32)
    return (key_part, value_part)


def general_shards(query_rows, key_rows, value_rows, lengths, out_weight, gate_vector, cotangent):
    tokens = query_rows.shape[1]
    local_width = query_rows.shape[2]
    head_count = local_width // HD
    score_scale = 1.0 / math.sqrt(HD)
    length = lengths[0]
    query_local = query_rows[0]
    key_local = key_rows[0]
    value_local = value_rows[0]
    query_heads = query_local.reshape(tokens, head_count, HD)
    key_heads = key_local.reshape(tokens, head_count, HD)
    value_heads = value_local.reshape(tokens, head_count, HD)
    head_zeros = jnp.zeros((tokens, head_count, HD), jnp.float32)
    start_top = jnp.full((tokens, head_count), MASKED_SCORE, jnp.float32)
    start_total = jnp.zeros((tokens, head_count), jnp.float32)
    key_piece = lax.all_gather(key_local, "seq", axis=0, tiled=True)
    value_piece = lax.all_gather(value_local, "seq", axis=0, tiled=True)
    piece_rows = key_piece.shape[0]
    step_rows = block_rows(piece_rows)

    def forward_block_step(block_index, state):
        row_top, row_total, summed = state
        offset = block_index * step_rows
        key_block = lax.dynamic_slice_in_dim(key_piece, offset, step_rows, 0).reshape(
            step_rows, head_count, HD
        )
        value_block = lax.dynamic_slice_in_dim(value_piece, offset, step_rows, 0).reshape(
            step_rows, head_count, HD
        )
        key_live = offset + jnp.arange(step_rows) < length
        scores = (
            jnp.einsum("thd,shd->ths", query_heads, key_block, preferred_element_type=jnp.float32)
            * score_scale
        )
        masked = jnp.where(key_live[None, None, :], scores, MASKED_SCORE)
        new_top = jnp.maximum(row_top, jnp.max(masked, axis=2))
        weights = jnp.where(key_live[None, None, :], jnp.exp(masked - new_top[:, :, None]), 0.0)
        shrink = jnp.exp(row_top - new_top)
        row_total = row_total * shrink + jnp.sum(weights, axis=2)
        summed = summed * shrink[:, :, None] + jnp.einsum(
            "ths,shd->thd",
            weights.astype(jnp.bfloat16),
            value_block,
            preferred_element_type=jnp.float32,
        )
        return (new_top, row_total, summed)

    row_top, row_total, summed = lax.fori_loop(
        0, piece_rows // step_rows, forward_block_step, (start_top, start_total, head_zeros)
    )
    attended_heads = (summed / row_total[:, :, None]).astype(jnp.bfloat16)
    attended = attended_heads.reshape(tokens, local_width)
    row_lse = row_top + jnp.log(row_total)
    weight_whole = lax.all_gather(out_weight, "seq", axis=0, tiled=True)
    partial_value = jnp.einsum(
        "tk,rk->tr", attended, weight_whole, preferred_element_type=jnp.float32
    )
    projected = lax.psum_scatter(
        partial_value.astype(jnp.bfloat16), "tensor", scatter_dimension=1, tiled=True
    ).astype(jnp.float32)
    out_width = projected.shape[1]
    gate_local = lax.dynamic_slice_in_dim(
        gate_vector[0], lax.axis_index("tensor") * out_width, out_width
    )
    cot_rows = cotangent[0].astype(jnp.float32)
    branch = (gate_local[None, :] * projected).astype(jnp.bfloat16)
    gate_grad = lax.psum(jnp.sum(cot_rows * projected, axis=0), "seq")
    grad_proj = (gate_local[None, :] * cot_rows).astype(jnp.bfloat16)
    grad_full = lax.all_gather(grad_proj, "tensor", axis=1, tiled=True)
    grad_att = jnp.dot(grad_full, weight_whole, preferred_element_type=jnp.float32).astype(
        jnp.bfloat16
    )
    row_share = lax.psum_scatter(
        jnp.einsum("tr,tk->rk", grad_full, attended, preferred_element_type=jnp.float32).astype(
            jnp.bfloat16
        ),
        "seq",
        scatter_dimension=0,
        tiled=True,
    )
    grad_weight = lax.psum(row_share, "dp").astype(jnp.float32)
    grad_heads = grad_att.reshape(tokens, head_count, HD)
    row_delta = jnp.sum(grad_heads.astype(jnp.float32) * attended_heads.astype(jnp.float32), axis=2)
    all_lse, all_delta = (
        lax.all_gather(row_lse, "seq", axis=0, tiled=True),
        lax.all_gather(row_delta, "seq", axis=0, tiled=True),
    )
    key_offset = lax.axis_index("seq") * tokens
    local_live = key_offset + jnp.arange(tokens) < length
    query_key_piece = lax.all_gather(key_local, "seq", axis=0, tiled=True)
    query_value_piece = lax.all_gather(value_local, "seq", axis=0, tiled=True)
    piece_rows = query_key_piece.shape[0]
    query_step_rows = block_rows(piece_rows)

    def query_block_step(block_index, state):
        offset = block_index * query_step_rows
        key_block = lax.dynamic_slice_in_dim(query_key_piece, offset, query_step_rows, 0).reshape(
            query_step_rows, head_count, HD
        )
        value_block = lax.dynamic_slice_in_dim(
            query_value_piece, offset, query_step_rows, 0
        ).reshape(query_step_rows, head_count, HD)
        key_live = offset + jnp.arange(query_step_rows) < length
        return state + query_terms(
            query_heads,
            grad_heads,
            row_lse,
            row_delta,
            key_block,
            value_block,
            key_live,
            score_scale,
        )

    grad_q = lax.fori_loop(0, piece_rows // query_step_rows, query_block_step, head_zeros)
    query_piece = lax.all_gather(query_local, "seq", axis=0, tiled=True)
    grad_piece = lax.all_gather(grad_att, "seq", axis=0, tiled=True)
    piece_rows = query_piece.shape[0]
    key_step_rows = block_rows(piece_rows)

    def key_block_step(block_index, state):
        offset = block_index * key_step_rows
        query_block = lax.dynamic_slice_in_dim(query_piece, offset, key_step_rows, 0).reshape(
            key_step_rows, head_count, HD
        )
        grad_block = lax.dynamic_slice_in_dim(grad_piece, offset, key_step_rows, 0).reshape(
            key_step_rows, head_count, HD
        )
        lse_block = lax.dynamic_slice_in_dim(all_lse, offset, key_step_rows, 0)
        delta_block = lax.dynamic_slice_in_dim(all_delta, offset, key_step_rows, 0)
        key_part, value_part = key_terms(
            query_block,
            grad_block,
            lse_block,
            delta_block,
            key_heads,
            value_heads,
            local_live,
            score_scale,
        )
        return (state[0] + key_part, state[1] + value_part)

    grad_k, grad_v = lax.fori_loop(
        0, piece_rows // key_step_rows, key_block_step, (head_zeros, head_zeros)
    )
    grad_query = grad_q.reshape(tokens, local_width).astype(jnp.bfloat16)
    grad_key = grad_k.reshape(tokens, local_width).astype(jnp.bfloat16)
    grad_value = grad_v.reshape(tokens, local_width).astype(jnp.bfloat16)
    return (
        branch[None],
        grad_query[None],
        grad_key[None],
        grad_value[None],
        grad_weight,
        gate_grad[None],
    )


VMEM_LIMIT = 40 * 1024 * 1024
NT = (((1,), (1,)), ((), ()))
TN = (((0,), (0,)), ((), ()))
NN = (((1,), (0,)), ((), ()))


def mm(left, right, dims):
    return lax.dot_general(left, right, dims, preferred_element_type=jnp.float32)


def lane_block(index, width):
    return pl.ds(pl.multiple_of(index * width, HD), width)


def call(kernel, out_shape, args, flops=0, smem=(), scratch=(), space=pltpu.VMEM, out_space=pltpu.VMEM, limit=VMEM_LIMIT):
    nbytes = sum(a.size * a.dtype.itemsize for a in args)
    nbytes += sum(math.prod(o.shape) * o.dtype.itemsize for o in jax.tree.leaves(out_shape))
    return pl.pallas_call(
        kernel,
        out_shape=out_shape,
        in_specs=[
            pl.BlockSpec(memory_space=pltpu.SMEM if i in smem else space)
            for i in range(len(args))
        ],
        out_specs=jax.tree.map(lambda _: pl.BlockSpec(memory_space=out_space), out_shape),
        scratch_shapes=list(scratch),
        compiler_params=pltpu.CompilerParams(vmem_limit_bytes=limit),
        cost_estimate=pl.CostEstimate(flops=flops, bytes_accessed=nbytes, transcendentals=0),
    )(*args)


def xor_pairs(count, k):
    return [(i, i ^ k) for i in range(count)]


def pack_kernel(q_ref, k_ref, v_ref, w_ref, kv_ref, q_own_ref, send_ref, near_ref, near2_ref, sems):
    s, core = lax.axis_index("seq"), lax.axis_index("dp")
    width, quarter = q_own_ref.shape[1], near_ref.shape[0]
    own, other = lane_block(s % 2, width), lane_block(1 - s % 2, width)
    pairs = [
        (k_ref.at[0, :, other], send_ref.at[0]),
        (v_ref.at[0, :, other], send_ref.at[1]),
        (q_ref.at[0, :, other], send_ref.at[2]),
        (k_ref.at[0, :, own], kv_ref.at[0]),
        (v_ref.at[0, :, own], kv_ref.at[1]),
        (q_ref.at[0, :, own], q_own_ref),
    ]
    for i, ref in enumerate((near_ref, near2_ref)):
        at = pl.multiple_of((2 * core + i) * quarter, quarter)
        pairs.append((w_ref.at[pl.ds(at, quarter), :], ref))
    copies = [pltpu.make_async_copy(a, b, sems.at[i]) for i, (a, b) in enumerate(pairs)]
    for copy in copies:
        copy.start()
    for copy in copies:
        copy.wait()


def head_rows(parts, head):
    return jnp.concatenate([p[:, head * HD : (head + 1) * HD] for p in parts], axis=0)


def live_bias(s, n, rows, length):
    parts = []
    for k in range(n):
        place = (s ^ k) * rows + lax.broadcasted_iota(jnp.int32, (rows, 1), 0)
        parts.append(jnp.where(place < length, 0.0, MASKED_SCORE))
    return jnp.concatenate(parts, axis=0)


def forward_kernel(n, scale, len_ref, *refs):
    kvs, queries, (o_ref, lse_ref) = refs[:n], (refs[n], refs[1].at[2]), refs[n + 1 :]
    s = lax.axis_index("seq")
    rows = o_ref.shape[1]
    bias = live_bias(s, n, rows, len_ref[0])
    for head in range(o_ref.shape[2] // HD):
        keys = head_rows([kv.at[0] for kv in kvs], head)
        values = head_rows([kv.at[1] for kv in kvs], head)
        scores = mm(keys, head_rows(queries, head), NT) * scale + bias
        top = jnp.max(scores, axis=0, keepdims=True)
        weights = jnp.exp(scores - top)
        total = jnp.sum(weights, axis=0, keepdims=True)
        summed = mm(values, weights.astype(jnp.bfloat16), TN)
        attended = (summed / total).T.astype(jnp.bfloat16)
        lse_ref[head : head + 1, :] = top + jnp.log(total)
        for u in range(2):
            o_ref[u, :, head * HD : (head + 1) * HD] = attended[u * rows : (u + 1) * rows]


def join_quarters(core, own_refs, other_refs, out_ref):
    rows = own_refs[0].shape[0]
    for i in range(2):
        at = pl.multiple_of((2 * core + i) * rows, rows)
        out_ref[pl.ds(at, rows), :] = own_refs[i][...]
        at = pl.multiple_of((2 * (1 - core) + i) * rows, rows)
        out_ref[pl.ds(at, rows), :] = other_refs[i][...]


def grad_attended_kernel(n, gate_ref, w_ref, *refs):
    quarters, cots, (own_ref, send_ref, cot_ref, w2_ref, share_ref) = refs[:4], refs[4 : 4 + n], refs[4 + n :]
    s = lax.axis_index("seq")
    rows, heads_width = own_ref.shape[1:]
    size = w_ref.shape[0]
    t = lax.axis_index("tensor")
    join_quarters(lax.axis_index("dp"), quarters[:2], quarters[2:], w2_ref)
    for k in range(n):
        cot_ref[s ^ t ^ k] = cots[k][0]
    total = None
    for b, weight_ref in ((0, w_ref), (1, w2_ref)):
        gate = gate_ref[:, lane_block(s ^ (2 * b), size)]
        cot = jnp.concatenate([cot_ref[2 * b], cot_ref[2 * b + 1]], axis=0)
        grad_proj = (gate * cot.astype(jnp.float32)).astype(jnp.bfloat16)
        part = mm(grad_proj, weight_ref[...], NN)
        total = part if total is None else total + part
    share_ref[...] = total
    own, other = lane_block(s % 2, heads_width), lane_block(1 - s % 2, heads_width)
    for u in range(2):
        own_ref[u] = share_ref[u * rows : (u + 1) * rows, own]
        send_ref[1 - u] = share_ref[u * rows : (u + 1) * rows, other].astype(jnp.bfloat16)


def backward_kernel(n, scale, len_ref, lse_ref, o_ref, own_ref, other_ref, *refs):
    kvs, queries = refs[:n], (refs[n], refs[1].at[2])
    dq_refs, dkv_refs = refs[n + 1 : n + 3], refs[n + 3 :]
    s = lax.axis_index("seq")
    rows = o_ref.shape[1]
    bias = live_bias(s, n, rows, len_ref[0])
    for head in range(o_ref.shape[2] // HD):
        lanes = slice(head * HD, (head + 1) * HD)
        keys = head_rows([kv.at[0] for kv in kvs], head)
        values = head_rows([kv.at[1] for kv in kvs], head)
        query = head_rows(queries, head)
        grad = jnp.concatenate(
            [own_ref[u, :, lanes] + other_ref[u, :, lanes].astype(jnp.float32) for u in range(2)],
            axis=0,
        ).astype(jnp.bfloat16)
        attended = jnp.concatenate([o_ref[u, :, lanes] for u in range(2)], axis=0)
        product = grad.astype(jnp.float32) * attended.astype(jnp.float32)
        delta = jnp.sum(product.T, axis=0, keepdims=True)
        scores = mm(keys, query, NT) * scale + bias
        probs = jnp.exp(scores - lse_ref[head : head + 1, :])
        grad_probs = mm(values, grad, NT)
        dscores = (probs * (grad_probs - delta) * scale).astype(jnp.bfloat16)
        grad_values = mm(probs.astype(jnp.bfloat16), grad, NN)
        grad_keys = mm(dscores, query, NN)
        grad_query = mm(keys, dscores, TN).T.astype(jnp.bfloat16)
        for u in range(2):
            dq_refs[u][:, lanes] = grad_query[u * rows : (u + 1) * rows]
        for k in range(n):
            out = dkv_refs[k]
            out[0, :, lanes] = grad_keys[k * rows : (k + 1) * rows].astype(out.dtype)
            out[1, :, lanes] = grad_values[k * rows : (k + 1) * rows].astype(out.dtype)


def forward_sum_kernel(own_ref, other_ref, out_ref):
    out_ref[...] = (own_ref[...] + other_ref[...].astype(jnp.float32)).astype(jnp.bfloat16)


def unpack_kernel(dq_ref, dq_other_ref, own_ref, part_ref, other_ref, *outs):
    s = lax.axis_index("seq")
    own, other = lane_block(s % 2, dq_ref.shape[1]), lane_block(1 - s % 2, dq_ref.shape[1])
    outs[0][0, :, own] = dq_ref[...]
    outs[0][0, :, other] = dq_other_ref[...]
    for i in range(2):
        total = own_ref[i] + part_ref[i].astype(jnp.float32)
        outs[1 + i][0, :, own] = total.astype(jnp.bfloat16)
        outs[1 + i][0, :, other] = other_ref[i]


def project_kernel(n, w_ref, w2_ref, o_ref, other_ref, *refs):
    (own_ref, *send_refs), (all_ref, parts_ref) = refs[:n], refs[n:]
    s, t = lax.axis_index("seq"), lax.axis_index("tensor")
    rows, heads_width = o_ref.shape[1:]
    own, other = lane_block(s % 2, heads_width), lane_block(1 - s % 2, heads_width)
    for u in range(2):
        all_ref[u * rows : (u + 1) * rows, own] = o_ref[u]
        all_ref[u * rows : (u + 1) * rows, other] = other_ref[1 - u]
    for b, weight_ref in ((0, w_ref), (1, w2_ref)):
        part = mm(all_ref[...], weight_ref[...], NT)
        for u in range(2):
            parts_ref[2 * b + u] = part[u * rows : (u + 1) * rows]
    own_ref[...] = parts_ref[s ^ t]
    for k in range(1, n):
        send_refs[k - 1][...] = parts_ref[s ^ t ^ k].astype(jnp.bfloat16)


def grad_weight_kernel(gate_ref, all_ref, cot_ref, keep_ref, send_ref, outer_ref):
    core, s = lax.axis_index("dp"), lax.axis_index("seq")
    size = all_ref.shape[1]
    half = size // 2
    for b in range(2):
        gate = gate_ref[:, lane_block(s ^ (2 * b), size)]
        cot = jnp.concatenate([cot_ref[2 * b], cot_ref[2 * b + 1]], axis=0)
        grad_proj = (gate * cot.astype(jnp.float32)).astype(jnp.bfloat16)
        outer_ref[...] = mm(grad_proj, all_ref[...], TN)
        keep_ref[b] = outer_ref[pl.ds(pl.multiple_of(core * half, half), half), :]
        send_ref[b] = outer_ref[pl.ds(pl.multiple_of((1 - core) * half, half), half), :].astype(
            jnp.bfloat16
        )


def weight_clips_kernel(keep_ref, other_ref, own_ref, send_ref):
    own_ref[...] = keep_ref[0] + other_ref[0].astype(jnp.float32)
    send_ref[...] = (keep_ref[1] + other_ref[1].astype(jnp.float32)).astype(jnp.bfloat16)


def weight_halves_kernel(own_ref, other_ref, out_ref):
    out_ref[...] = (own_ref[...] + other_ref[...].astype(jnp.float32)).astype(jnp.bfloat16)


def weight_join_kernel(own_ref, other_ref, out_ref):
    core = lax.axis_index("dp")
    half = own_ref.shape[0]
    own = pl.ds(pl.multiple_of(core * half, half), half)
    out_ref[own, :] = own_ref[...].astype(jnp.float32)
    other = pl.ds(pl.multiple_of((1 - core) * half, half), half)
    out_ref[other, :] = other_ref[...].astype(jnp.float32)


def projected_kernel(n, own_ref, *refs):
    parts, out_ref = refs[: n - 1], refs[n - 1]
    projected = own_ref[...]
    for part in parts:
        projected = projected + part[...].astype(jnp.float32)
    out_ref[...] = projected.astype(jnp.bfloat16)


def branch_kernel(gate_ref, cot_ref, projected_ref, branch_ref, gate_grad_ref):
    projected = projected_ref[...].astype(jnp.float32)
    gate = gate_ref[:, lane_block(lax.axis_index("tensor"), projected.shape[1])]
    branch_ref[0] = (gate * projected).astype(jnp.bfloat16)
    cot = cot_ref[0].astype(jnp.float32)
    gate_grad = jnp.sum(cot * projected, axis=0, keepdims=True)
    for i in range(gate_grad_ref.shape[0]):
        gate_grad_ref[i] = gate_grad


def square_shards(
    n, query_rows, key_rows, value_rows, lengths, out_weight, gate_vector, cotangent
):
    tokens, width = query_rows.shape[1:]
    scale = 1.0 / math.sqrt(HD)
    bf16, f32 = jnp.bfloat16, jnp.float32
    shape = jax.ShapeDtypeStruct
    both = ("seq", "tensor")
    both_pairs = [(a, b) for a in range(n) for b in range(n)]

    def permute(value, axes, k):
        return lax.ppermute(value, axes, xor_pairs(n, k))

    def swap(value):
        return lax.ppermute(value, "dp", xor_pairs(2, 1))

    width_half = width // 2
    rows_kv, rows_q = (2, tokens, width_half), (tokens, width_half)
    kv, query, send, near_a, near_b = call(
        pack_kernel,
        [
            shape(rows_kv, bf16),
            shape(rows_q, bf16),
            shape((3, tokens, width_half), bf16),
            *[shape((width_half // 2, width), bf16)] * 2,
        ],
        (query_rows, key_rows, value_rows, out_weight),
        scratch=[pltpu.SemaphoreType.DMA((8,))],
        space=pl.ANY,
        limit=60 * 1024 * 1024,
    )

    def turn(value, k):
        return lax.ppermute(
            value,
            both,
            [
                (a * n + b, ((a & 2) | (b & 1)) * n + (b ^ k ^ ((a ^ b) & 1)))
                for a, b in both_pairs
            ],
        )

    qkv_x, kv_y, near_a, cot_1, cot_2, near_b, cot_late = lax.optimization_barrier(
        (
            permute(send, "seq", 1),
            permute(kv, "seq", 2),
            permute(near_a, "seq", 2),
            turn(cotangent, 1),
            turn(cotangent, 2),
            near_b,
            cotangent,
        )
    )
    kv_xy = permute(qkv_x[:2], "seq", 2)
    kvs = (kv, qkv_x, kv_y, kv_xy)
    block = 2 * tokens
    unit_flops = 2 * n * tokens * block * HD
    wide_flops = 4 * block * width * width
    attended, lse = call(
        functools.partial(forward_kernel, n, scale),
        [shape(rows_kv, bf16), shape((width_half // HD, block), f32)],
        (lengths, *kvs, query),
        flops=6 * unit_flops,
        smem=(0,),
    )
    near_b, attended = lax.optimization_barrier((permute(near_b, "seq", 2), attended))
    far_a = swap(near_a)
    cots = (turn(cot_late, 0), cot_1, cot_2, turn(cot_late, 3))
    heads = (attended, permute(attended, "seq", 1))
    grad_own, grad_send, cot_all, weight_y = call(
        functools.partial(grad_attended_kernel, n),
        [
            shape(rows_kv, f32),
            shape(rows_kv, bf16),
            shape((n, tokens, width), bf16),
            shape((width, width), bf16),
        ],
        (gate_vector, out_weight, near_a, near_b, far_a, swap(near_b), *cots),
        flops=wide_flops,
        scratch=[pltpu.VMEM((block, width), f32)],
    )
    grad_other = permute(grad_send, "seq", 1)
    *parts, attended_all = call(
        functools.partial(project_kernel, n),
        [
            shape((tokens, width), f32),
            *[shape((tokens, width), bf16)] * (n - 1),
            shape((block, width), bf16),
        ],
        (out_weight, weight_y, *heads),
        flops=wide_flops,
        scratch=[pltpu.VMEM((n, tokens, width), f32)],
    )
    dq, dq_send, dkv, dkv_x, dkv_y, dkv_xy = call(
        functools.partial(backward_kernel, n, scale),
        [shape(rows_q, bf16)] * 2 + [shape(rows_kv, f32)] * 2 + [shape(rows_kv, bf16)] * 2,
        (lengths, lse, attended, grad_own, grad_other, *kvs, query),
        flops=15 * unit_flops,
        smem=(0,),
    )
    keep, send = call(
        grad_weight_kernel,
        [shape((2, width_half, width), f32), shape((2, width_half, width), bf16)],
        (gate_vector, attended_all, cot_all),
        flops=wide_flops,
        scratch=[pltpu.VMEM((width, width), f32)],
    )
    parts = [parts[0]] + [permute(parts[k], "tensor", k) for k in range(1, n)]
    own, send = call(
        weight_clips_kernel,
        [shape((width_half, width), f32), shape((width_half, width), bf16)],
        (keep, swap(send)),
    )
    fin = call(
        weight_halves_kernel, shape((width_half, width), bf16), (own, permute(send, "seq", 2))
    )
    grad_weight = call(weight_join_kernel, shape((width, width), f32), (fin, swap(fin)))
    dq_other, dkv_xy = permute(dq_send, "seq", 1), permute(dkv_xy, "seq", 2)
    dkv_y = permute(dkv_y, "seq", 2)
    dkv_xy, dq_other = lax.optimization_barrier((dkv_xy, dq_other))
    dkv_x = call(forward_sum_kernel, shape(rows_kv, bf16), (dkv_x, dkv_xy))
    dkv_other = permute(dkv_x, "seq", 1)
    projected = call(
        functools.partial(projected_kernel, n), shape((tokens, width), bf16), tuple(parts)
    )
    home = [(a * n + b, (a ^ 1) * n + (b ^ 1) if (a ^ b) & 1 else a * n + b) for a, b in both_pairs]
    projected = lax.ppermute(projected, both, home)
    projected, grad_weight = lax.optimization_barrier((projected, grad_weight))
    branch, grad_gate = call(
        branch_kernel,
        [shape((1, tokens, width), bf16), shape((n, 1, width), f32)],
        (gate_vector, cotangent, projected),
    )
    grad_gate = jnp.sum(lax.all_to_all(grad_gate, "seq", 0, 0, tiled=True), axis=0)
    grad_query, grad_key, grad_value = call(
        unpack_kernel,
        [shape((1, tokens, width), bf16)] * 3,
        (dq, dq_other, dkv, dkv_y, dkv_other),
    )
    return (branch, grad_query, grad_key, grad_value, grad_weight, grad_gate)


def solution(mesh):
    placed = (
        P("dp", "seq", "tensor"),
        P("dp", "seq", "tensor"),
        P("dp", "seq", "tensor"),
        P("dp"),
        P("seq", "tensor"),
        P("dp", None),
        P("dp", "seq", "tensor"),
    )
    n = mesh.shape["seq"]

    def body(query_rows, *rest):
        tokens, width = query_rows.shape[1:]
        square = (
            n == 4
            and mesh.shape["tensor"] == n
            and mesh.shape["dp"] == 2
            and width % (2 * HD) == 0
            and tokens % 32 == 0
        )
        if square:
            return square_shards(n, query_rows, *rest)
        return general_shards(query_rows, *rest)

    return jax.shard_map(
        body,
        mesh=mesh,
        in_specs=placed,
        out_specs=(
            P("dp", "seq", "tensor"),
            P("dp", "seq", "tensor"),
            P("dp", "seq", "tensor"),
            P("dp", "seq", "tensor"),
            P("seq", "tensor"),
            P("dp", "tensor"),
        ),
        check_vma=False,
    )
```
